32 devices in a mesh: groups: 2 (over y), aperture: 4 (over z), beam: 2 (over x), range: 2 (over core).
Axes of the slice: x: 2, y: 2, z: 4, core: 2. Of those that a mesh axis runs over, the one named last changes fastest.
Arguments:
- echoes: bfloat16 [2, 2048, 1024], P(None, ('groups', 'aperture', 'beam'), 'range'), parts along dimension 1, may hold values from -6 to 6
- chirp_taps: bfloat16 [2, 64], replicated, may hold values from -0.75 to 0.75
- steer_phase: float32 [256, 512], P(None, 'beam'), may hold values from -3.140625 to 3.140625
- ang_table: int32 [2, 2, 2, 512], P(None, None, None, 'beam'), may hold values from 0 to 255
- range_table: int32 [2, 2, 2, 512], P(None, None, None, 'beam'), may hold values from -13 to 12
- interp_taps: float32 [2, 2, 2, 2, 8, 512], P(None, None, None, None, None, 'beam'), may hold values from -1 to 1
- phase_twist: float32 [2, 2, 2, 512], P(None, None, None, 'beam'), may hold values from -12 to 12
Outputs:
- scene_image: float32 [8, 2, 512, 1024], P(('groups', 'aperture'), None, 'beam', 'range'), parts along dimension 0
The draws below stay inside these ranges and needn't reach their ends.
There are 2 independent parts, one for each index of `groups`. The reference program is written for one: setup_inputs(seed, part) draws one part's arguments, and reference() takes and returns one part's arrays. A program takes and returns all parts, laid end to end along the dimension named above; an argument that names none is the same for every part. Nothing has to cross between parts.
Inputs may be any that keep to these rules, and one draw needn't show every extreme that they name: `ang_table`: entry (l, h, c, j) counts from the first beam of the block of 256 beams that holds beam j.
All inputs are finite; a program needn't handle non-finite values.
Results may differ from the reference program's by a relative error of at most 0.0037.
Values may be sent and summed in bfloat16 or wider, within the bound.
No kernel may reach another device: no remote copies, remote signals or barrier semaphores. Data moves between devices by JAX's collectives and lax.ppermute only.
A program may use at most 128 MiB of HBM per device.

```python
import jax
import jax.numpy as jnp
from jax import lax

BEAM_DEV = 256
CHIRP_LEN = 64
INTERP_LEN = 8
RIM_CELLS = 16
SUB_PULSES = 256
PULSES = 1024
BEAM_COUNT = 512
RANGE_BINS = 1024
LEVELS = 2
N_APERTURE = 4


def place_ends(result, key, least, largest):
    place = [jax.random.randint(jax.random.fold_in(key, axis), (), 0, length) for axis, length in enumerate(result.shape)]
    main_axis = result.shape.index(max(result.shape))
    beside = place[:main_axis] + [(place[main_axis] + 1) % result.shape[main_axis]] + place[main_axis + 1:]
    return result.at[tuple(place)].set(least).at[tuple(beside)].set(largest)


def levels(rng, dims, cuts, smallest, largest):
    loudness = 1.0
    for position, parts in cuts:
        steps = jax.random.uniform(jax.random.fold_in(jax.random.fold_in(rng, 6), position), (parts,), jnp.float32, smallest / len(cuts), largest / len(cuts))
        loudness = loudness * jnp.repeat(jnp.exp(steps), dims[position] // parts).reshape((-1,) + (1,) * (len(dims) - 1 - position))
    return loudness


def normal_values(key, shape, spread, limit, cuts=(), kind=jnp.bfloat16):
    array = spread * jax.random.normal(key, shape, jnp.float32)
    if cuts:
        array = array * levels(key, shape, cuts, -0.22, 0.18)
    return jnp.clip(array, -limit, limit).astype(kind)


def setup_inputs(seed: int = 0, part: int = 0) -> dict:
    splits = jax.random.split(jax.random.key(seed), 8)
    part_splits = jax.random.split(jax.random.fold_in(splits[7], part), 8)
    return {
        "echoes": normal_values(part_splits[0], (2, PULSES, RANGE_BINS), 1.0, 6.0, ((1, 8), (2, 2))),
        "chirp_taps": normal_values(splits[1], (2, CHIRP_LEN), CHIRP_LEN ** -0.5, 0.75),
        "steer_phase": jnp.clip(jax.random.uniform(splits[2], (SUB_PULSES, BEAM_COUNT), jnp.float32, -3.140625, 3.140625), -3.140625, 3.140625),
        "ang_table": place_ends(jax.random.randint(splits[3], (LEVELS, 2, 2, BEAM_COUNT), 0, BEAM_DEV), jax.random.fold_in(splits[3], 1), 0, BEAM_DEV - 1).astype(jnp.int32),
        "range_table": place_ends(jax.random.randint(splits[4], (LEVELS, 2, 2, BEAM_COUNT), INTERP_LEN // 2 - 1 - RIM_CELLS, RIM_CELLS - INTERP_LEN // 2 + 1), jax.random.fold_in(splits[4], 1), INTERP_LEN // 2 - 1 - RIM_CELLS, (RIM_CELLS - INTERP_LEN // 2 + 1) - 1).astype(jnp.int32),
        "interp_taps": normal_values(splits[5], (LEVELS, 2, 2, 2, INTERP_LEN, BEAM_COUNT), 32 ** -0.5, 1.0, ((5, 2),), jnp.float32),
        "phase_twist": jnp.clip(jax.random.uniform(splits[6], (LEVELS, 2, 2, BEAM_COUNT), jnp.float32, -12.0, 12.0) * levels(splits[6], (LEVELS, 2, 2, BEAM_COUNT), ((3, 2),), -0.4, 0.0), -12.0, 12.0),
    }


def contribute(extended, angles, offsets, weights, rates, fraction):
    range_width = fraction.shape[0]
    starts = offsets + (RIM_CELLS - INTERP_LEN // 2 + 1)
    zero_index = jnp.zeros((), jnp.int32)

    def pick_window(beam_index, start_index):
        return lax.dynamic_slice(extended, (zero_index, beam_index, start_index), (2, 1, range_width + INTERP_LEN - 1))[:, 0, :]

    windows = jax.vmap(pick_window, out_axes=1)(angles, starts)
    real_part = jnp.zeros((angles.shape[0], range_width), jnp.float32)
    imag_part = jnp.zeros((angles.shape[0], range_width), jnp.float32)
    for tap_index in range(INTERP_LEN):
        tap_real = weights[0, tap_index][:, None]
        tap_imag = weights[1, tap_index][:, None]
        part_real = windows[0, :, tap_index:tap_index + range_width]
        part_imag = windows[1, :, tap_index:tap_index + range_width]
        real_part = real_part + tap_real * part_real - tap_imag * part_imag
        imag_part = imag_part + tap_real * part_imag + tap_imag * part_real
    rot_angle = rates[:, None] * fraction[None, :]
    cosine = jnp.cos(rot_angle)
    sine_value = jnp.sin(rot_angle)
    return jnp.stack([real_part * cosine - imag_part * sine_value, real_part * sine_value + imag_part * cosine])


def reference(echoes, chirp_taps, steer_phase, ang_table, range_table, interp_taps, phase_twist):
    echo_real = echoes[0].astype(jnp.float32)
    echo_imag = echoes[1].astype(jnp.float32)
    padding = jnp.zeros((PULSES, CHIRP_LEN), jnp.float32)
    ext_real = jnp.concatenate([echo_real, padding], axis=1)
    ext_imag = jnp.concatenate([echo_imag, padding], axis=1)
    chirp_real = chirp_taps[0].astype(jnp.float32)
    chirp_imag = chirp_taps[1].astype(jnp.float32)

    def tap_step(tap_index, totals):
        tap_index = tap_index.astype(jnp.int32)
        shifted_real = lax.dynamic_slice_in_dim(ext_real, tap_index, RANGE_BINS, 1)
        shifted_imag = lax.dynamic_slice_in_dim(ext_imag, tap_index, RANGE_BINS, 1)
        coeff_real = lax.dynamic_index_in_dim(chirp_real, tap_index, keepdims=False)
        coeff_imag = lax.dynamic_index_in_dim(chirp_imag, tap_index, keepdims=False)
        return (totals[0] + coeff_real * shifted_real + coeff_imag * shifted_imag,
                totals[1] + coeff_real * shifted_imag - coeff_imag * shifted_real)

    zero_field = jnp.zeros((PULSES, RANGE_BINS), jnp.float32)
    sums_real, sums_imag = lax.fori_loop(0, CHIRP_LEN, tap_step, (zero_field, zero_field))
    compressed = jnp.stack([sums_real, sums_imag]).astype(jnp.bfloat16)

    steer_scale = SUB_PULSES ** -0.5
    cos_table = (jnp.cos(steer_phase) * steer_scale).astype(jnp.bfloat16)
    sin_table = (-jnp.sin(steer_phase) * steer_scale).astype(jnp.bfloat16)
    slot_list = jnp.arange(N_APERTURE, dtype=jnp.int32)

    def form_slot(slot_index):
        block_rows = lax.dynamic_slice_in_dim(compressed, slot_index * SUB_PULSES, SUB_PULSES, 1)
        real_part = (jnp.dot(cos_table.T, block_rows[0], preferred_element_type=jnp.float32)
                     - jnp.dot(sin_table.T, block_rows[1], preferred_element_type=jnp.float32))
        imag_part = (jnp.dot(cos_table.T, block_rows[1], preferred_element_type=jnp.float32)
                     + jnp.dot(sin_table.T, block_rows[0], preferred_element_type=jnp.float32))
        return jnp.stack([real_part, imag_part])

    images = lax.map(form_slot, slot_list)
    fraction = jnp.arange(RANGE_BINS, dtype=jnp.int32).astype(jnp.float32) / RANGE_BINS
    block_start = (jnp.arange(BEAM_COUNT, dtype=jnp.int32) // BEAM_DEV) * BEAM_DEV

    for level_index in range(LEVELS):
        def merge_slot(slot_index, level_index=level_index, images=images):
            own_half = (slot_index >> level_index) & 1
            merged = None
            for child_bit in (0, 1):
                child_slot = (slot_index & ~(1 << level_index)) | (child_bit << level_index)
                padded = jnp.pad(images[child_slot], ((0, 0), (0, 0), (RIM_CELLS, RIM_CELLS)))
                term = contribute(padded,
                                  block_start + ang_table[level_index, own_half, child_bit],
                                  range_table[level_index, own_half, child_bit],
                                  interp_taps[level_index, own_half, child_bit],
                                  phase_twist[level_index, own_half, child_bit],
                                  fraction)
                merged = term if merged is None else merged + term
            return merged

        images = lax.map(merge_slot, slot_list)
    return images
```

```python
import functools

import jax
import jax.numpy as jnp
from jax import lax
from jax.experimental import pallas as pl
from jax.experimental.pallas import tpu as pltpu
from jax.sharding import PartitionSpec as P

INTERP_LEN = 8
RIM_CELLS = 16


def from_behind(value, axis, steps):
    count = lax.axis_size(axis)
    leading, last = (max(0, -steps), min(count, count - steps))
    return lax.ppermute(value, axis, [(source, source + steps) for source in range(leading, last)])


def with_halo(x, sides, width):
    for axis, dim in sides:
        peers, length = (lax.axis_size(axis), x.shape[dim])
        up = [(i, (i + 1) % peers) for i in range(peers - 1)]
        down = [(j, i) for i, j in up]
        last = lax.slice_in_dim(x, length - width, length, axis=dim)
        leading = lax.slice_in_dim(x, 0, width, axis=dim)
        before = lax.ppermute(last, axis, up)
        after = lax.ppermute(leading, axis, down)
        x = jnp.concatenate([before, x, after], axis=dim)
    return x


def swapped(value, axis, stride):
    mask = 2**stride
    pairs = [(source, source ^ mask) for source in range(lax.axis_size(axis))]
    return lax.ppermute(value, axis, pairs)


def transposed_dot(left_side, right_side):
    return lax.dot_general(
        left_side, right_side, (((0,), (0,)), ((), ())), preferred_element_type=jnp.float32
    )


def toeplitz_matrix(chirp_taps):
    tap_count = chirp_taps.shape[1]
    row_index = lax.broadcasted_iota(jnp.int32, (128 + tap_count, 128), 0)
    col_index = lax.broadcasted_iota(jnp.int32, (128 + tap_count, 128), 1)
    lag_index = row_index - col_index
    tap_index = lax.iota(jnp.int32, tap_count)
    tap_hits = (lag_index[:, :, None] == tap_index[None, None, :]).astype(jnp.float32)
    real_part = jnp.sum(tap_hits * chirp_taps[0].astype(jnp.float32), axis=2)
    imag_part = jnp.sum(tap_hits * chirp_taps[1].astype(jnp.float32), axis=2)
    upper_half = jnp.concatenate([real_part, -imag_part], axis=1)
    lower_half = jnp.concatenate([imag_part, real_part], axis=1)
    return jnp.concatenate([upper_half, lower_half], axis=0).astype(jnp.bfloat16)


def compress(main_cols, upper_rim, kernel):
    piece_rows = main_cols.shape[1]
    range_width = main_cols.shape[2]
    tap_count = upper_rim.shape[2]
    blocks = range_width // 128
    filler = jnp.zeros((2, piece_rows, 128 - tap_count), main_cols.dtype)
    padded = jnp.concatenate([main_cols, upper_rim, filler], axis=2)
    head_cols = padded[:, :, :range_width].reshape(2, piece_rows, blocks, 128)
    tail_cols = padded[:, :, 128 : range_width + 128].reshape(2, piece_rows, blocks, 128)[
        :, :, :, :tap_count
    ]
    windows = jnp.concatenate([head_cols, tail_cols], axis=3)
    row_blocks = jnp.transpose(windows, (1, 2, 0, 3)).reshape(
        piece_rows * blocks, 2 * (128 + tap_count)
    )
    result = jnp.dot(row_blocks, kernel, preferred_element_type=jnp.float32)
    result = result.reshape(piece_rows, blocks, 2, 128)
    return (
        jnp.transpose(result, (2, 0, 1, 3)).reshape(2, piece_rows, range_width).astype(jnp.bfloat16)
    )


def contribute(extended, angles, offsets, weights, rates, fraction):
    range_width = fraction.shape[0]
    span = 2 * RIM_CELLS + 1
    picked = jnp.take(extended, angles, axis=1)
    shift_list = lax.iota(jnp.int32, span) - RIM_CELLS
    tap_list = lax.iota(jnp.int32, INTERP_LEN)
    lag_table = offsets[None, :] + tap_list[:, None] - (INTERP_LEN // 2 - 1)
    hits = (lag_table[None, :, :] == shift_list[:, None, None]).astype(jnp.float32)
    spread_real = jnp.sum(hits * weights[0][None, :, :], axis=1)
    spread_imag = jnp.sum(hits * weights[1][None, :, :], axis=1)
    real_part = jnp.zeros((angles.shape[0], range_width), jnp.float32)
    imag_part = jnp.zeros((angles.shape[0], range_width), jnp.float32)
    for shift_index in range(span):
        tap_real = spread_real[shift_index][:, None]
        tap_imag = spread_imag[shift_index][:, None]
        part_real = picked[0, :, shift_index : shift_index + range_width]
        part_imag = picked[1, :, shift_index : shift_index + range_width]
        real_part = real_part + tap_real * part_real - tap_imag * part_imag
        imag_part = imag_part + tap_real * part_imag + tap_imag * part_real
    rot_angle = rates[:, None] * fraction[None, :]
    cosine = jnp.cos(rot_angle)
    sine_value = jnp.sin(rot_angle)
    return jnp.stack(
        [real_part * cosine - imag_part * sine_value, real_part * sine_value + imag_part * cosine]
    )


def level_by_level(echoes, chirp_taps, steer_phase, ang_table, range_table, interp_taps, phase_twist):
    tap_count = chirp_taps.shape[1]
    kernel = toeplitz_matrix(chirp_taps)
    upper_rim = from_behind(echoes[:, :, :tap_count], "range", -1)
    sub_rows = steer_phase.shape[0]
    range_width = echoes.shape[2]
    steer_scale = sub_rows ** (-0.5)
    cos_table = (jnp.cos(steer_phase) * steer_scale).astype(jnp.bfloat16)
    sin_table = (-jnp.sin(steer_phase) * steer_scale).astype(jnp.bfloat16)
    compressed = compress(echoes, upper_rim, kernel)
    shard_rows = lax.all_gather(compressed, "beam", axis=1, tiled=True)
    real_part = transposed_dot(cos_table, shard_rows[0]) - transposed_dot(sin_table, shard_rows[1])
    imag_part = transposed_dot(cos_table, shard_rows[1]) + transposed_dot(sin_table, shard_rows[0])
    images = jnp.stack([real_part, imag_part])
    slot_index = lax.axis_index("aperture")
    level_count = lax.axis_size("aperture").bit_length() - 1
    range_total = range_width * lax.axis_size("range")
    fraction = (lax.axis_index("range") * range_width + lax.iota(jnp.int32, range_width)).astype(
        jnp.float32
    ) / range_total
    for level_index in range(level_count):
        own_half = slot_index >> level_index & 1
        far_half = 1 - own_half
        extended = with_halo(images, (("range", 2),), RIM_CELLS)
        own_share = contribute(
            extended,
            ang_table[level_index, own_half, own_half],
            range_table[level_index, own_half, own_half],
            interp_taps[level_index, own_half, own_half],
            phase_twist[level_index, own_half, own_half],
            fraction,
        )
        partner_image = swapped(extended, "aperture", level_index)
        images = own_share + contribute(
            partner_image,
            ang_table[level_index, own_half, far_half],
            range_table[level_index, own_half, far_half],
            interp_taps[level_index, own_half, far_half],
            phase_twist[level_index, own_half, far_half],
            fraction,
        )
    return images[None]


LANES = 128
SUBS = 8
STEP = 16
SPAN = 2 * RIM_CELLS


def merge_tables(level, own_half, range_table, interp_taps, phase_twist, first_bin, half_bins, total):
    steps = half_bins // STEP
    sign = jnp.array([1.0, -1.0], jnp.float32).reshape(2, 1, 1, 1)

    def rows(x):
        lead = x.shape[:-1]
        x = x.reshape(lead + (1, 1, 2, LANES))
        return jnp.broadcast_to(x, lead + (2, 2, 2, LANES))

    taps = rows(interp_taps[level, own_half])
    phase = rows(phase_twist[level, own_half]) * sign
    within = (lax.iota(jnp.int32, STEP).astype(jnp.float32) / total).reshape(STEP, 1, 1, 1, 1)
    start = first_bin + lax.broadcasted_iota(jnp.int32, (steps, 1, 2, 1, 1), 0) * STEP
    start = start + lax.broadcasted_iota(jnp.int32, (steps, 1, 2, 1, 1), 2) * half_bins
    start = start.astype(jnp.float32) / total
    near, far = phase[:, None] * within, phase[:, None] * start
    table = jnp.concatenate(
        [taps[:, 0], taps[:, 1] * sign, jnp.cos(near), jnp.sin(near), jnp.cos(far), jnp.sin(far)],
        axis=1,
    )
    table = table.reshape(2, table.shape[1], SUBS, LANES)
    shift = rows(range_table[level, own_half] + (RIM_CELLS - INTERP_LEN // 2 + 1))
    return table, shift.reshape(2, SUBS, LANES)


def squeeze(parts, sibling, core, near_mat, edge_mat, c_ref, index):
    bins = parts[0].shape[-1]

    def columns(low, high):
        found = []
        for own, other in zip(parts, sibling):
            tiles = []
            for tile in range(low, high):
                if tile == 0:
                    rim = other[:, bins - LANES :]
                    tiles.append(jnp.where(core == 1, rim, jnp.zeros_like(rim)))
                elif tile == bins // LANES + 1:
                    rim = other[:, :LANES]
                    tiles.append(jnp.where(core == 0, rim, jnp.zeros_like(rim)))
                else:
                    tiles.append(own[:, (tile - 1) * LANES : tile * LANES])
            found += tiles
        return jnp.concatenate(found, axis=1)

    def times(matrix, cols):
        return lax.dot_general(
            matrix, cols, (((1,), (1,)), ((), ())), preferred_element_type=jnp.float32
        )

    for block in range(bins // LANES + 2):
        if block == 0:
            rows = jnp.concatenate([near_mat[LANES - SPAN : LANES], near_mat[2 * LANES - SPAN :]], 0)
            result = times(rows, columns(0, 2))
            result = jnp.where(core == 1, result, 0.0).astype(jnp.bfloat16)
            place, count = 0, SPAN
        elif block <= bins // LANES:
            result = times(near_mat[...], columns(block, block + 2)).astype(jnp.bfloat16)
            place, count = SPAN + (block - 1) * LANES, LANES
        else:
            result = times(edge_mat[...], columns(block, block + 1)).astype(jnp.bfloat16)
            place, count = SPAN + bins, SPAN
        c_ref[index, 0, place : place + count] = result[:count]
        c_ref[index, 1, place : place + count] = result[count:]


def form(c_ref, slot, steer_ref, x_ref):
    pieces = [c_ref[slot * 2 + x, ri] for ri in (0, 1) for x in (0, 1)]
    image = jnp.dot(
        jnp.concatenate(pieces, axis=1), steer_ref[...], preferred_element_type=jnp.float32
    ).astype(jnp.bfloat16)
    beams = x_ref.shape[2]
    x_ref[0] = image[:, :beams]
    x_ref[1] = image[:, beams:]


def merge_child(x_ref, ang, shift, table, child, s_ref, y_ref, o_ref, half_bins, fresh):
    beams = x_ref.shape[2]
    beam_index = lax.broadcasted_iota(jnp.int32, (beams, beams), 0)
    hits = jnp.where(beam_index == ang[child], 1.0, 0.0).astype(jnp.bfloat16)
    length = half_bins + SPAN
    for ri in (0, 1):
        picked = jnp.dot(x_ref[ri], hits, preferred_element_type=jnp.float32)
        for half in (0, 1):
            for part in (0, 1):
                s_ref[pl.ds(ri * 4 + half * 2 + part, length, stride=SUBS), :] = picked[
                    half * half_bins : half * half_bins + length, part * LANES : (part + 1) * LANES
                ]
    offset = shift[child]
    bits = [(offset & (1 << b)) != 0 for b in range(5)]

    def align(step, carry):
        base = pl.multiple_of(step * (STEP * SUBS), STEP * SUBS)
        row = [s_ref[pl.ds(base + k * SUBS, SUBS), :] for k in range(STEP + 31)]
        for b in (4, 3, 2, 1, 0):
            d = 1 << b
            row = [jnp.where(bits[b], row[k + d], row[k]) for k in range(len(row) - d)]
        for k in range(STEP):
            y_ref[pl.ds(base + k * SUBS, SUBS), :] = row[k]
        return carry

    lax.fori_loop(0, half_bins // STEP + 1, align, 0)
    taps = INTERP_LEN
    near, far = 2 * taps, 2 * taps + 2 * STEP
    steps = half_bins // STEP

    def weigh(step, carry):
        base = pl.multiple_of(step * (STEP * SUBS), STEP * SUBS)
        far_r, far_i = table[child, far + step], table[child, far + steps + step]
        w_r, w_i = [], []
        for t in range(taps):
            a, b = table[child, t], table[child, taps + t]
            w_r.append(a * far_r - b * far_i)
            w_i.append(a * far_i + b * far_r)
        for low in range(0, STEP, SUBS):
            row = [y_ref[pl.ds(base + (low + k) * SUBS, SUBS), :] for k in range(SUBS + taps - 1)]
            for k in range(SUBS):
                a, b = row[k] * w_r[0], row[k] * w_i[0]
                for t in range(1, taps):
                    a = a + row[k + t] * w_r[t]
                    b = b + row[k + t] * w_i[t]
                e_r, e_i = table[child, near + low + k], table[child, near + STEP + low + k]
                value = (e_r * a - e_i * b) + pltpu.roll(e_i * a + e_r * b, SUBS // 2, 0)
                place = pl.ds(base + (low + k) * SUBS, SUBS)
                o_ref[place, :] = value if fresh else o_ref[place, :] + value
        return carry

    lax.fori_loop(0, steps, weigh, 0)


def merged_image(o_ref, x_ref, half_bins, first_bin, total):
    for half in (0, 1):
        bin_index = lax.broadcasted_iota(jnp.int32, (half_bins, 2 * LANES), 0)
        bin_index = bin_index + (first_bin + half * half_bins)
        inside = (bin_index >= 0) & (bin_index < total)
        for ri in (0, 1):
            value = jnp.concatenate(
                [
                    o_ref[pl.ds(ri * 4 + half * 2 + part, half_bins, stride=SUBS), :]
                    for part in (0, 1)
                ],
                axis=1,
            )
            x_ref[ri, half * half_bins : (half + 1) * half_bins] = jnp.where(
                inside, value, 0.0
            ).astype(jnp.bfloat16)


def finished(o_ref, out_ref, half_bins):
    for ri in (0, 1):
        for half in (0, 1):
            for part in (0, 1):
                value = o_ref[pl.ds(ri * 4 + half * 2 + part, half_bins, stride=SUBS), :]
                out_ref[
                    0, ri, part * LANES : (part + 1) * LANES, half * half_bins : (half + 1) * half_bins
                ] = value.T


def all_kernel(*refs, total):
    meta = refs[0]
    pieces, siblings = refs[1:10], refs[10:19]
    near_mat, edge_mat, steer, ang, shift, table0, table1 = refs[19:26]
    out_ref = refs[26]
    c_ref, x0_ref, x1_ref, s_ref, y_ref, o0_ref, o1_ref = refs[27:]
    core = meta[0]
    bins = out_ref.shape[3]
    whole = lambda ref: [ref.at[0], ref.at[1]]
    for i in range(8):
        if i < 7:
            own, other = whole(pieces[i]), whole(siblings[i])
        else:
            own, other = [pieces[7].at[0], pieces[8].at[0]], [siblings[7].at[0], siblings[8].at[0]]
        squeeze(own, other, core, near_mat, edge_mat, c_ref, meta[3 + i])
    half0, half1 = (bins + SPAN) // 2, bins // 2
    for top in (0, 1):
        for low in (0, 1):
            form(c_ref, top * 2 + low, steer, x0_ref)
            merge_child(x0_ref, ang.at[0], shift.at[0], table0, low, s_ref, y_ref, o0_ref, half0, low == 0)
        merged_image(o0_ref, x1_ref, half0, core * bins - RIM_CELLS, total)
        merge_child(x1_ref, ang.at[1], shift.at[1], table1, top, s_ref, y_ref, o1_ref, half1, top == 0)
    finished(o1_ref, out_ref, half1)


def ring_of_chips(echoes, chirp_taps, steer_phase, ang_table, range_table, interp_taps, phase_twist):
    pulses, bins = echoes.shape[1:]
    beams = steer_phase.shape[1]
    total = bins * lax.axis_size("range")
    slots = lax.axis_size("aperture")
    slot, column, core = (lax.axis_index(a) for a in ("aperture", "beam", "range"))
    axes = ("aperture", "beam")
    order = [z * 2 for z in range(slots)] + [z * 2 + 1 for z in reversed(range(slots))]
    ahead = [(order[i], order[(i + 1) % len(order)]) for i in range(len(order))]
    behind = [(b, a) for a, b in ahead]
    place = jnp.where(column == 0, slot, 2 * slots - 1 - slot)

    up = down = echoes
    pieces = [echoes]
    sources = [place]
    for step in range(1, slots):
        up, down = lax.ppermute(up, axes, ahead), lax.ppermute(down, axes, behind)
        pieces += [up, down]
        sources += [place - step, place + step]
    pieces += [lax.ppermute(up[:1], axes, ahead), lax.ppermute(down[1:], axes, behind)]
    sources.append(place + slots)
    siblings = [lax.ppermute(x, "range", [(0, 1), (1, 0)]) for x in pieces]
    ring = jnp.stack(sources) % (2 * slots)
    ring = jnp.where(ring < slots, 2 * ring, 2 * (2 * slots - 1 - ring) + 1)
    meta = jnp.concatenate([jnp.stack([core, slot & 1, slot >> 1]), ring]).astype(jnp.int32)

    lag = lax.broadcasted_iota(jnp.int32, (LANES, 2 * LANES), 1)
    lag = lag - lax.broadcasted_iota(jnp.int32, (LANES, 2 * LANES), 0)
    hits = (lag[:, :, None] == lax.iota(jnp.int32, chirp_taps.shape[1])).astype(jnp.float32)
    t_r, t_i = (jnp.sum(hits * chirp_taps[i].astype(jnp.float32), axis=2) for i in (0, 1))
    near_mat = jnp.block([[t_r, t_i], [-t_i, t_r]]).astype(jnp.bfloat16)
    e_r, e_i = t_r[:SPAN, :LANES], t_i[:SPAN, :LANES]
    edge_mat = jnp.block([[e_r, e_i], [-e_i, e_r]]).astype(jnp.bfloat16)
    scale = steer_phase.shape[0] ** (-0.5)
    cos_table = (jnp.cos(steer_phase) * scale).astype(jnp.bfloat16)
    sin_table = (-jnp.sin(steer_phase) * scale).astype(jnp.bfloat16)
    steer = jnp.block([[cos_table, sin_table], [-sin_table, cos_table]])
    halves = (slot & 1, slot >> 1 & 1)
    half0, half1 = (bins + SPAN) // 2, bins // 2
    first = core * bins
    table0, shift0 = merge_tables(
        0, halves[0], range_table, interp_taps, phase_twist, first - RIM_CELLS, half0, total
    )
    table1, shift1 = merge_tables(
        1, halves[1], range_table, interp_taps, phase_twist, first, half1, total
    )
    shift = jnp.stack([shift0, shift1])
    ang = jnp.stack([ang_table[level, halves[level]] for level in (0, 1)])[:, :, None, :]

    vmem = pl.BlockSpec(memory_space=pltpu.VMEM)
    rows = half0 + SPAN + 32
    window = bins + 2 * SPAN
    return pl.pallas_call(
        functools.partial(all_kernel, total=total),
        out_shape=jax.ShapeDtypeStruct((1, 2, beams, bins), jnp.float32),
        in_specs=[pl.BlockSpec(memory_space=pltpu.SMEM)] + [vmem] * 25,
        out_specs=vmem,
        scratch_shapes=[
            pltpu.VMEM((2 * slots, 2, window, pulses), jnp.bfloat16),
            pltpu.VMEM((2, window, beams), jnp.bfloat16),
            pltpu.VMEM((2, window - SPAN, beams), jnp.bfloat16),
            pltpu.VMEM((rows * SUBS, LANES), jnp.float32),
            pltpu.VMEM((rows * SUBS, LANES), jnp.float32),
            pltpu.VMEM((half0 * SUBS, LANES), jnp.float32),
            pltpu.VMEM((half1 * SUBS, LANES), jnp.float32),
        ],
        compiler_params=pltpu.CompilerParams(vmem_limit_bytes=40 * 1024 * 1024),
        name="backproject",
    )(meta, *pieces, *siblings, near_mat, edge_mat, steer, ang, shift, table0, table1)


def solution(mesh):
    small = (mesh.shape["aperture"], mesh.shape["beam"], mesh.shape["range"]) == (4, 2, 2)
    return jax.shard_map(
        ring_of_chips if small else level_by_level,
        mesh=mesh,
        in_specs=(
            P(None, ("groups", "aperture", "beam"), "range"),
            P(),
            P(None, "beam"),
            P(None, None, None, "beam"),
            P(None, None, None, "beam"),
            P(None, None, None, None, None, "beam"),
            P(None, None, None, "beam"),
        ),
        out_specs=P(("groups", "aperture"), None, "beam", "range"),
        check_vma=False,
    )
```

```python
import functools

import jax
import jax.numpy as jnp
from jax import lax
from jax.experimental import pallas as pl
from jax.experimental.pallas import tpu as pltpu
from jax.sharding import PartitionSpec as P

INTERP_LEN = 8
RIM_CELLS = 16


def from_behind(value, axis, steps):
    count = lax.axis_size(axis)
    leading, last = (max(0, -steps), min(count, count - steps))
    return lax.ppermute(value, axis, [(source, source + steps) for source in range(leading, last)])


def with_halo(x, sides, width):
    for axis, dim in sides:
        peers, length = (lax.axis_size(axis), x.shape[dim])
        up = [(i, (i + 1) % peers) for i in range(peers - 1)]
        down = [(j, i) for i, j in up]
        last = lax.slice_in_dim(x, length - width, length, axis=dim)
        leading = lax.slice_in_dim(x, 0, width, axis=dim)
        before = lax.ppermute(last, axis, up)
        after = lax.ppermute(leading, axis, down)
        x = jnp.concatenate([before, x, after], axis=dim)
    return x


def swapped(value, axis, stride):
    mask = 2**stride
    pairs = [(source, source ^ mask) for source in range(lax.axis_size(axis))]
    return lax.ppermute(value, axis, pairs)


def transposed_dot(left_side, right_side):
    return lax.dot_general(
        left_side, right_side, (((0,), (0,)), ((), ())), preferred_element_type=jnp.float32
    )


def toeplitz_matrix(chirp_taps):
    tap_count = chirp_taps.shape[1]
    row_index = lax.broadcasted_iota(jnp.int32, (128 + tap_count, 128), 0)
    col_index = lax.broadcasted_iota(jnp.int32, (128 + tap_count, 128), 1)
    lag_index = row_index - col_index
    tap_index = lax.iota(jnp.int32, tap_count)
    tap_hits = (lag_index[:, :, None] == tap_index[None, None, :]).astype(jnp.float32)
    real_part = jnp.sum(tap_hits * chirp_taps[0].astype(jnp.float32), axis=2)
    imag_part = jnp.sum(tap_hits * chirp_taps[1].astype(jnp.float32), axis=2)
    upper_half = jnp.concatenate([real_part, -imag_part], axis=1)
    lower_half = jnp.concatenate([imag_part, real_part], axis=1)
    return jnp.concatenate([upper_half, lower_half], axis=0).astype(jnp.bfloat16)


def compress(main_cols, upper_rim, kernel):
    piece_rows = main_cols.shape[1]
    range_width = main_cols.shape[2]
    tap_count = upper_rim.shape[2]
    blocks = range_width // 128
    filler = jnp.zeros((2, piece_rows, 128 - tap_count), main_cols.dtype)
    padded = jnp.concatenate([main_cols, upper_rim, filler], axis=2)
    head_cols = padded[:, :, :range_width].reshape(2, piece_rows, blocks, 128)
    tail_cols = padded[:, :, 128 : range_width + 128].reshape(2, piece_rows, blocks, 128)[
        :, :, :, :tap_count
    ]
    windows = jnp.concatenate([head_cols, tail_cols], axis=3)
    row_blocks = jnp.transpose(windows, (1, 2, 0, 3)).reshape(
        piece_rows * blocks, 2 * (128 + tap_count)
    )
    result = jnp.dot(row_blocks, kernel, preferred_element_type=jnp.float32)
    result = result.reshape(piece_rows, blocks, 2, 128)
    return (
        jnp.transpose(result, (2, 0, 1, 3)).reshape(2, piece_rows, range_width).astype(jnp.bfloat16)
    )


def contribute(extended, angles, offsets, weights, rates, fraction):
    range_width = fraction.shape[0]
    span = 2 * RIM_CELLS + 1
    picked = jnp.take(extended, angles, axis=1)
    shift_list = lax.iota(jnp.int32, span) - RIM_CELLS
    tap_list = lax.iota(jnp.int32, INTERP_LEN)
    lag_table = offsets[None, :] + tap_list[:, None] - (INTERP_LEN // 2 - 1)
    hits = (lag_table[None, :, :] == shift_list[:, None, None]).astype(jnp.float32)
    spread_real = jnp.sum(hits * weights[0][None, :, :], axis=1)
    spread_imag = jnp.sum(hits * weights[1][None, :, :], axis=1)
    real_part = jnp.zeros((angles.shape[0], range_width), jnp.float32)
    imag_part = jnp.zeros((angles.shape[0], range_width), jnp.float32)
    for shift_index in range(span):
        tap_real = spread_real[shift_index][:, None]
        tap_imag = spread_imag[shift_index][:, None]
        part_real = picked[0, :, shift_index : shift_index + range_width]
        part_imag = picked[1, :, shift_index : shift_index + range_width]
        real_part = real_part + tap_real * part_real - tap_imag * part_imag
        imag_part = imag_part + tap_real * part_imag + tap_imag * part_real
    rot_angle = rates[:, None] * fraction[None, :]
    cosine = jnp.cos(rot_angle)
    sine_value = jnp.sin(rot_angle)
    return jnp.stack(
        [real_part * cosine - imag_part * sine_value, real_part * sine_value + imag_part * cosine]
    )


def level_by_level(echoes, chirp_taps, steer_phase, ang_table, range_table, interp_taps, phase_twist):
    tap_count = chirp_taps.shape[1]
    kernel = toeplitz_matrix(chirp_taps)
    upper_rim = from_behind(echoes[:, :, :tap_count], "range", -1)
    sub_rows = steer_phase.shape[0]
    range_width = echoes.shape[2]
    steer_scale = sub_rows ** (-0.5)
    cos_table = (jnp.cos(steer_phase) * steer_scale).astype(jnp.bfloat16)
    sin_table = (-jnp.sin(steer_phase) * steer_scale).astype(jnp.bfloat16)
    compressed = compress(echoes, upper_rim, kernel)
    shard_rows = lax.all_gather(compressed, "beam", axis=1, tiled=True)
    real_part = transposed_dot(cos_table, shard_rows[0]) - transposed_dot(sin_table, shard_rows[1])
    imag_part = transposed_dot(cos_table, shard_rows[1]) + transposed_dot(sin_table, shard_rows[0])
    images = jnp.stack([real_part, imag_part])
    slot_index = lax.axis_index("aperture")
    level_count = lax.axis_size("aperture").bit_length() - 1
    range_total = range_width * lax.axis_size("range")
    fraction = (lax.axis_index("range") * range_width + lax.iota(jnp.int32, range_width)).astype(
        jnp.float32
    ) / range_total
    for level_index in range(level_count):
        own_half = slot_index >> level_index & 1
        far_half = 1 - own_half
        extended = with_halo(images, (("range", 2),), RIM_CELLS)
        own_share = contribute(
            extended,
            ang_table[level_index, own_half, own_half],
            range_table[level_index, own_half, own_half],
            interp_taps[level_index, own_half, own_half],
            phase_twist[level_index, own_half, own_half],
            fraction,
        )
        partner_image = swapped(extended, "aperture", level_index)
        images = own_share + contribute(
            partner_image,
            ang_table[level_index, own_half, far_half],
            range_table[level_index, own_half, far_half],
            interp_taps[level_index, own_half, far_half],
            phase_twist[level_index, own_half, far_half],
            fraction,
        )
    return images[None]


LANES = 128
SUBS = 8
STEP = 16
SPAN = 2 * RIM_CELLS
NEAR = 2 * INTERP_LEN
FAR = NEAR + 2 * STEP


def table_kernel(meta, chirp, phase, ang, offset, taps, twist, near_mat, edge_mat, steer, *outs, total):
    core, slot, column = meta[0], meta[1], meta[2]
    bins = total // 2
    pulses = phase.shape[0] // 2
    beams = phase.shape[1]
    shape = (LANES, 2 * LANES)
    t_r, t_i = (
        pltpu.roll(jnp.broadcast_to(chirp[i : i + 1, :], shape), 0, 1, stride=1, stride_axis=0)
        for i in (0, 1)
    )
    for matrix, rows, cols in ((near_mat, LANES, 2 * LANES), (edge_mat, SPAN, LANES)):
        real, imag = t_r[:rows, :cols].astype(jnp.bfloat16), t_i[:rows, :cols].astype(jnp.bfloat16)
        matrix[:rows, :cols] = real
        matrix[:rows, cols:] = imag
        matrix[rows:, :cols] = -imag
        matrix[rows:, cols:] = real
    scale = phase.shape[0] ** (-0.5)
    for x in (0, 1):
        half = column ^ x
        angle = phase[pl.ds(pl.multiple_of(half * pulses, pulses), pulses), :]
        cos_part = (jnp.cos(angle) * scale).astype(jnp.bfloat16)
        sin_part = (-jnp.sin(angle) * scale).astype(jnp.bfloat16)
        low, high = x * pulses, (x + 1) * pulses
        steer[low:high, :beams] = cos_part
        steer[low:high, beams:] = sin_part
        steer[2 * pulses + low : 2 * pulses + high, :beams] = -sin_part
        steer[2 * pulses + low : 2 * pulses + high, beams:] = cos_part
    sub = lax.broadcasted_iota(jnp.int32, (SUBS, LANES), 0)

    def rows(line):
        return jnp.where((sub & 1) == 0, line[:, :LANES], line[:, LANES:])

    sign = jnp.where(sub < SUBS // 2, 1.0, -1.0)
    ang_out, shift_out = outs[0], outs[1]
    todo = []
    for level in (0, 1):
        table = outs[2 + level]
        own = (slot >> level) & 1
        for order in (0, 1):
            child = own if order == 0 else 1 - own
            ang_out[level, order] = ang[level, own, pl.ds(child, 1), :]
            shift_out[level, order] = rows(offset[level, own, pl.ds(child, 1), :]) + (
                RIM_CELLS - INTERP_LEN // 2 + 1
            )
            for t in range(INTERP_LEN):
                table[order, t] = rows(taps[level, own, child, 0, t : t + 1, :])
                table[order, INTERP_LEN + t] = sign * rows(taps[level, own, child, 1, t : t + 1, :])
            rate = sign * rows(twist[level, own, pl.ds(child, 1), :])
            half_bins = (bins + SPAN) // 2 if level == 0 else bins // 2
            first = core * bins + ((sub >> 1) & 1) * half_bins
            first = first - RIM_CELLS if level == 0 else first
            todo.append((table, order, rate, first, half_bins // STEP))

    def turn(step, carry):
        for table, order, rate, first, steps in todo:
            near = rate * (step.astype(jnp.float32) / total)
            table[order, NEAR + step] = jnp.cos(near)
            table[order, NEAR + STEP + step] = jnp.sin(near)
            far = rate * ((first + STEP * step).astype(jnp.float32) / total)
            table[order, FAR + step] = jnp.cos(far)
            table[order, FAR + steps + step] = jnp.sin(far)
        return carry

    lax.fori_loop(0, STEP, turn, 0)
    for table, order, rate, first, steps in todo:
        for step in range(STEP, steps):
            far = rate * ((first + STEP * step).astype(jnp.float32) / total)
            table[order, FAR + step] = jnp.cos(far)
            table[order, FAR + steps + step] = jnp.sin(far)


def squeeze(piece, rim, core, near_mat, edge_mat, c_ref, index):
    bins = piece.shape[-1]

    def columns(low, high):
        found = []
        for ri in (0, 1):
            tiles = []
            for tile in range(low, high):
                if tile == 0:
                    other = rim[ri, :, bins - LANES :]
                    tiles.append(jnp.where(core == 1, other, jnp.zeros_like(other)))
                elif tile == bins // LANES + 1:
                    other = rim[ri, :, :LANES]
                    tiles.append(jnp.where(core == 0, other, jnp.zeros_like(other)))
                else:
                    tiles.append(piece[ri, :, (tile - 1) * LANES : tile * LANES])
            found += tiles
        return jnp.concatenate(found, axis=1)

    def times(matrix, cols):
        return lax.dot_general(
            matrix, cols, (((1,), (1,)), ((), ())), preferred_element_type=jnp.float32
        )

    for block in range(bins // LANES + 2):
        if block == 0:
            rows = jnp.concatenate([near_mat[LANES - SPAN : LANES], near_mat[2 * LANES - SPAN :]], 0)
            result = times(rows, columns(0, 2))
            result = jnp.where(core == 1, result, 0.0).astype(jnp.bfloat16)
            place, count = 0, SPAN
        elif block <= bins // LANES:
            result = times(near_mat[...], columns(block, block + 2)).astype(jnp.bfloat16)
            place, count = SPAN + (block - 1) * LANES, LANES
        else:
            result = times(edge_mat[...], columns(block, block + 1)).astype(jnp.bfloat16)
            place, count = SPAN + bins, SPAN
        c_ref[index, 0, place : place + count] = result[:count]
        c_ref[index, 1, place : place + count] = result[count:]


def form(c_ref, steer, x_ref):
    pieces = [c_ref[i, ri] for ri in (0, 1) for i in (0, 1)]
    image = jnp.dot(
        jnp.concatenate(pieces, axis=1), steer[...], preferred_element_type=jnp.float32
    ).astype(jnp.bfloat16)
    beams = x_ref.shape[2]
    x_ref[0] = image[:, :beams]
    x_ref[1] = image[:, beams:]


def merge_child(x_ref, ang, shift, table, s_ref, y_ref, base_ref, o_ref, half_bins):
    beams = x_ref.shape[2]
    beam_index = lax.broadcasted_iota(jnp.int32, (beams, beams), 0)
    hits = jnp.where(beam_index == ang[...], 1.0, 0.0).astype(jnp.bfloat16)
    length = half_bins + SPAN
    for ri in (0, 1):
        picked = jnp.dot(x_ref[ri], hits, preferred_element_type=jnp.float32)
        for half in (0, 1):
            for part in (0, 1):
                s_ref[pl.ds(ri * 4 + half * 2 + part, length, stride=SUBS), :] = picked[
                    half * half_bins : half * half_bins + length, part * LANES : (part + 1) * LANES
                ]
    offset = shift[...]
    bits = [(offset & (1 << b)) != 0 for b in range(5)]
    steps = half_bins // STEP
    for step in range(steps + 1):
        base = step * STEP
        row = [s_ref[pl.ds((base + k) * SUBS, SUBS), :] for k in range(STEP + 31)]
        for b in (4, 3, 2, 1, 0):
            d = 1 << b
            row = [jnp.where(bits[b], row[k + d], row[k]) for k in range(len(row) - d)]
        for k in range(STEP):
            y_ref[pl.ds((base + k) * SUBS, SUBS), :] = row[k]
    taps = INTERP_LEN
    for step in range(steps):
        far_r, far_i = table[FAR + step], table[FAR + steps + step]
        w_r, w_i = [], []
        for t in range(taps):
            a, b = table[t], table[taps + t]
            w_r.append(a * far_r - b * far_i)
            w_i.append(a * far_i + b * far_r)
        for low in range(0, STEP, SUBS):
            base = step * STEP + low
            row = [y_ref[pl.ds((base + k) * SUBS, SUBS), :] for k in range(SUBS + taps - 1)]
            for k in range(SUBS):
                a, b = row[k] * w_r[0], row[k] * w_i[0]
                for t in range(1, taps):
                    a = a + row[k + t] * w_r[t]
                    b = b + row[k + t] * w_i[t]
                e_r, e_i = table[NEAR + low + k], table[NEAR + STEP + low + k]
                value = (e_r * a - e_i * b) + pltpu.roll(e_i * a + e_r * b, SUBS // 2, 0)
                place = pl.ds((base + k) * SUBS, SUBS)
                o_ref[place, :] = value if base_ref is None else base_ref[place, :] + value


def merged_image(o_ref, x_ref, half_bins, first_bin, total):
    for half in (0, 1):
        bin_index = lax.broadcasted_iota(jnp.int32, (half_bins, 2 * LANES), 0)
        bin_index = bin_index + (first_bin + half * half_bins)
        inside = (bin_index >= 0) & (bin_index < total)
        for ri in (0, 1):
            value = jnp.concatenate(
                [
                    o_ref[pl.ds(ri * 4 + half * 2 + part, half_bins, stride=SUBS), :]
                    for part in (0, 1)
                ],
                axis=1,
            )
            x_ref[ri, half * half_bins : (half + 1) * half_bins] = jnp.where(
                inside, value, 0.0
            ).astype(jnp.bfloat16)


def finished(o_ref, out_ref, half_bins):
    for ri in (0, 1):
        for half in (0, 1):
            for part in (0, 1):
                value = o_ref[pl.ds(ri * 4 + half * 2 + part, half_bins, stride=SUBS), :]
                out_ref[
                    0, ri, part * LANES : (part + 1) * LANES, half * half_bins : (half + 1) * half_bins
                ] = value.T


def stage_kernel(stage, total, *refs):
    (meta, first, first_rim, second, second_rim, near_mat, edge_mat, steer, ang, shift, table0) = refs[:11]
    refs = refs[11:]
    core = meta[0]
    bins = total // 2
    half0, half1 = (bins + SPAN) // 2, bins // 2
    order = stage & 1
    table1 = base0 = base1 = None
    if order == 1:
        table1, base0, refs = refs[0], refs[1], refs[2:]
    if stage == 3:
        base1, refs = refs[0], refs[1:]
    out_ref, c_ref, x0_ref, s_ref, y_ref = refs[:5]
    squeeze(first, first_rim, core, near_mat, edge_mat, c_ref, 0)
    squeeze(second, second_rim, core, near_mat, edge_mat, c_ref, 1)
    form(c_ref, steer, x0_ref)
    o_ref = out_ref if order == 0 else refs[5]
    merge_child(
        x0_ref, ang.at[0, order], shift.at[0, order], table0.at[order], s_ref, y_ref, base0, o_ref, half0
    )
    if order == 0:
        return
    x1_ref = refs[6]
    merged_image(o_ref, x1_ref, half0, core * bins - RIM_CELLS, total)
    which = stage >> 1
    final = out_ref if stage == 1 else refs[7]
    merge_child(
        x1_ref, ang.at[1, which], shift.at[1, which], table1.at[which], s_ref, y_ref, base1, final, half1
    )
    if stage == 3:
        finished(final, out_ref, half1)


def ring_of_chips(echoes, chirp_taps, steer_phase, ang_table, range_table, interp_taps, phase_twist):
    pulses, bins = echoes.shape[1:]
    beams = steer_phase.shape[1]
    total = bins * lax.axis_size("range")
    slots = lax.axis_size("aperture")
    slot, column, core = (lax.axis_index(a) for a in ("aperture", "beam", "range"))
    axes = ("aperture", "beam")
    order = [z * 2 for z in range(slots)] + [z * 2 + 1 for z in reversed(range(slots))]
    ahead = [(order[i], order[(i + 1) % len(order)]) for i in range(len(order))]
    behind = [(b, a) for a, b in ahead]
    across = [(2 * z + x, 2 * z + 1 - x) for z in range(1, slots - 1) for x in (0, 1)]
    kind = jnp.where(column == 0, slot, slots - 1 - slot)
    half0, half1 = (bins + SPAN) // 2, bins // 2
    window = bins + 2 * SPAN
    meta = jnp.stack([core, slot, column]).astype(jnp.int32)

    def other_core(x):
        return lax.ppermute(x, "range", [(0, 1), (1, 0)])

    def choose(*options):
        picked = options[-1]
        for value, option in enumerate(options[:-1]):
            if option is not picked:
                picked = jnp.where(kind == value, option, picked)
        return picked

    smem, vmem = pl.BlockSpec(memory_space=pltpu.SMEM), pl.BlockSpec(memory_space=pltpu.VMEM)
    f32, bf16, i32 = jnp.float32, jnp.bfloat16, jnp.int32
    rows0 = NEAR + 2 * STEP + 2 * (half0 // STEP)
    rows1 = NEAR + 2 * STEP + 2 * (half1 // STEP)
    chirp = jnp.pad(chirp_taps.astype(f32), ((0, 0), (0, 2 * LANES - chirp_taps.shape[1])))
    tables = pl.pallas_call(
        functools.partial(table_kernel, total=total),
        out_shape=[
            jax.ShapeDtypeStruct((2 * LANES, 4 * LANES), bf16),
            jax.ShapeDtypeStruct((2 * SPAN, 2 * LANES), bf16),
            jax.ShapeDtypeStruct((4 * pulses, 2 * beams), bf16),
            jax.ShapeDtypeStruct((2, 2, 1, beams), i32),
            jax.ShapeDtypeStruct((2, 2, SUBS, LANES), i32),
            jax.ShapeDtypeStruct((2, rows0, SUBS, LANES), f32),
            jax.ShapeDtypeStruct((2, rows1, SUBS, LANES), f32),
        ],
        in_specs=[smem] + [vmem] * 6,
        out_specs=[vmem] * 7,
        compiler_params=pltpu.CompilerParams(vmem_limit_bytes=16 * 1024 * 1024),
        cost_estimate=pl.CostEstimate(flops=10**9, bytes_accessed=4 * 2**20, transcendentals=0),
        name="tables",
    )(meta, chirp, steer_phase, ang_table, range_table, interp_taps, phase_twist)
    shared, table0, table1 = tables[:5], tables[5], tables[6]

    def run(stage, first, second, *carried):
        rows = (half0 + SPAN + 32) * SUBS
        if stage == 3:
            out = jax.ShapeDtypeStruct((1, 2, beams, bins), f32)
        else:
            out = jax.ShapeDtypeStruct(((half1 if stage == 1 else half0) * SUBS, LANES), f32)
        scratch = [
            pltpu.VMEM((2, 2, window, pulses), bf16),
            pltpu.VMEM((2, window, beams), bf16),
            pltpu.VMEM((rows, LANES), f32),
            pltpu.VMEM((rows, LANES), f32),
        ]
        if stage & 1:
            scratch.append(pltpu.VMEM((half0 * SUBS, LANES), f32))
            scratch.append(pltpu.VMEM((2, window - SPAN, beams), bf16))
        if stage == 3:
            scratch.append(pltpu.VMEM((half1 * SUBS, LANES), f32))
        given = [meta, first[0], first[1], second[0], second[1], *shared, table0, *carried]
        return pl.pallas_call(
            functools.partial(stage_kernel, stage, total),
            out_shape=out,
            in_specs=[smem] + [vmem] * (len(given) - 1),
            out_specs=vmem,
            scratch_shapes=scratch,
            compiler_params=pltpu.CompilerParams(vmem_limit_bytes=24 * 1024 * 1024),
            cost_estimate=pl.CostEstimate(
                flops=3 * 10**9, bytes_accessed=4 * 2**20, transcendentals=0
            ),
            name=f"stage{stage}",
        )(*given)

    up1, down1 = lax.ppermute(echoes, axes, ahead), lax.ppermute(echoes, axes, behind)
    side = lax.ppermute(echoes, axes, across)
    up2, down2 = lax.ppermute(up1, axes, ahead), lax.ppermute(down1, axes, behind)
    up3, down3 = lax.ppermute(up2, axes, ahead), lax.ppermute(down2, axes, behind)
    far = jnp.concatenate(
        [lax.ppermute(up3[:1], axes, ahead), lax.ppermute(down3[1:], axes, behind)], axis=0
    )
    pair = lambda x: (x, other_core(x))
    part = run(0, pair(echoes), pair(choose(up1, side, side, down1)))
    near = run(
        1, pair(choose(down1, up1, down1, up1)), pair(choose(up2, up2, down2, down2)), table1, part
    )
    part = run(2, pair(choose(down2, down2, up2, up2)), pair(choose(up3, down3, up3, down3)))
    return run(3, pair(choose(down3, down1, up1, up3)), pair(far), table1, part, near)


def solution(mesh):
    small = (mesh.shape["aperture"], mesh.shape["beam"], mesh.shape["range"]) == (4, 2, 2)
    return jax.shard_map(
        ring_of_chips if small else level_by_level,
        mesh=mesh,
        in_specs=(
            P(None, ("groups", "aperture", "beam"), "range"),
            P(),
            P(None, "beam"),
            P(None, None, None, "beam"),
            P(None, None, None, "beam"),
            P(None, None, None, None, None, "beam"),
            P(None, None, None, "beam"),
        ),
        out_specs=P(("groups", "aperture"), None, "beam", "range"),
        check_vma=False,
    )
```

```python
import functools

import jax
import jax.numpy as jnp
from jax import lax
from jax.experimental import pallas as pl
from jax.experimental.pallas import tpu as pltpu
from jax.sharding import PartitionSpec as P

INTERP_LEN = 8
RIM_CELLS = 16


def from_behind(value, axis, steps):
    count = lax.axis_size(axis)
    leading, last = (max(0, -steps), min(count, count - steps))
    return lax.ppermute(value, axis, [(source, source + steps) for source in range(leading, last)])


def with_halo(x, sides, width):
    for axis, dim in sides:
        peers, length = (lax.axis_size(axis), x.shape[dim])
        up = [(i, (i + 1) % peers) for i in range(peers - 1)]
        down = [(j, i) for i, j in up]
        last = lax.slice_in_dim(x, length - width, length, axis=dim)
        leading = lax.slice_in_dim(x, 0, width, axis=dim)
        before = lax.ppermute(last, axis, up)
        after = lax.ppermute(leading, axis, down)
        x = jnp.concatenate([before, x, after], axis=dim)
    return x


def swapped(value, axis, stride):
    mask = 2**stride
    pairs = [(source, source ^ mask) for source in range(lax.axis_size(axis))]
    return lax.ppermute(value, axis, pairs)


def transposed_dot(left_side, right_side):
    return lax.dot_general(
        left_side, right_side, (((0,), (0,)), ((), ())), preferred_element_type=jnp.float32
    )


def toeplitz_matrix(chirp_taps):
    tap_count = chirp_taps.shape[1]
    row_index = lax.broadcasted_iota(jnp.int32, (128 + tap_count, 128), 0)
    col_index = lax.broadcasted_iota(jnp.int32, (128 + tap_count, 128), 1)
    lag_index = row_index - col_index
    tap_index = lax.iota(jnp.int32, tap_count)
    tap_hits = (lag_index[:, :, None] == tap_index[None, None, :]).astype(jnp.float32)
    real_part = jnp.sum(tap_hits * chirp_taps[0].astype(jnp.float32), axis=2)
    imag_part = jnp.sum(tap_hits * chirp_taps[1].astype(jnp.float32), axis=2)
    upper_half = jnp.concatenate([real_part, -imag_part], axis=1)
    lower_half = jnp.concatenate([imag_part, real_part], axis=1)
    return jnp.concatenate([upper_half, lower_half], axis=0).astype(jnp.bfloat16)


def compress(main_cols, upper_rim, kernel):
    piece_rows = main_cols.shape[1]
    range_width = main_cols.shape[2]
    tap_count = upper_rim.shape[2]
    blocks = range_width // 128
    filler = jnp.zeros((2, piece_rows, 128 - tap_count), main_cols.dtype)
    padded = jnp.concatenate([main_cols, upper_rim, filler], axis=2)
    head_cols = padded[:, :, :range_width].reshape(2, piece_rows, blocks, 128)
    tail_cols = padded[:, :, 128 : range_width + 128].reshape(2, piece_rows, blocks, 128)[
        :, :, :, :tap_count
    ]
    windows = jnp.concatenate([head_cols, tail_cols], axis=3)
    row_blocks = jnp.transpose(windows, (1, 2, 0, 3)).reshape(
        piece_rows * blocks, 2 * (128 + tap_count)
    )
    result = jnp.dot(row_blocks, kernel, preferred_element_type=jnp.float32)
    result = result.reshape(piece_rows, blocks, 2, 128)
    return (
        jnp.transpose(result, (2, 0, 1, 3)).reshape(2, piece_rows, range_width).astype(jnp.bfloat16)
    )


def contribute(extended, angles, offsets, weights, rates, fraction):
    range_width = fraction.shape[0]
    span = 2 * RIM_CELLS + 1
    picked = jnp.take(extended, angles, axis=1)
    shift_list = lax.iota(jnp.int32, span) - RIM_CELLS
    tap_list = lax.iota(jnp.int32, INTERP_LEN)
    lag_table = offsets[None, :] + tap_list[:, None] - (INTERP_LEN // 2 - 1)
    hits = (lag_table[None, :, :] == shift_list[:, None, None]).astype(jnp.float32)
    spread_real = jnp.sum(hits * weights[0][None, :, :], axis=1)
    spread_imag = jnp.sum(hits * weights[1][None, :, :], axis=1)
    real_part = jnp.zeros((angles.shape[0], range_width), jnp.float32)
    imag_part = jnp.zeros((angles.shape[0], range_width), jnp.float32)
    for shift_index in range(span):
        tap_real = spread_real[shift_index][:, None]
        tap_imag = spread_imag[shift_index][:, None]
        part_real = picked[0, :, shift_index : shift_index + range_width]
        part_imag = picked[1, :, shift_index : shift_index + range_width]
        real_part = real_part + tap_real * part_real - tap_imag * part_imag
        imag_part = imag_part + tap_real * part_imag + tap_imag * part_real
    rot_angle = rates[:, None] * fraction[None, :]
    cosine = jnp.cos(rot_angle)
    sine_value = jnp.sin(rot_angle)
    return jnp.stack(
        [real_part * cosine - imag_part * sine_value, real_part * sine_value + imag_part * cosine]
    )


def level_by_level(echoes, chirp_taps, steer_phase, ang_table, range_table, interp_taps, phase_twist):
    tap_count = chirp_taps.shape[1]
    kernel = toeplitz_matrix(chirp_taps)
    upper_rim = from_behind(echoes[:, :, :tap_count], "range", -1)
    sub_rows = steer_phase.shape[0]
    range_width = echoes.shape[2]
    steer_scale = sub_rows ** (-0.5)
    cos_table = (jnp.cos(steer_phase) * steer_scale).astype(jnp.bfloat16)
    sin_table = (-jnp.sin(steer_phase) * steer_scale).astype(jnp.bfloat16)
    compressed = compress(echoes, upper_rim, kernel)
    shard_rows = lax.all_gather(compressed, "beam", axis=1, tiled=True)
    real_part = transposed_dot(cos_table, shard_rows[0]) - transposed_dot(sin_table, shard_rows[1])
    imag_part = transposed_dot(cos_table, shard_rows[1]) + transposed_dot(sin_table, shard_rows[0])
    images = jnp.stack([real_part, imag_part])
    slot_index = lax.axis_index("aperture")
    level_count = lax.axis_size("aperture").bit_length() - 1
    range_total = range_width * lax.axis_size("range")
    fraction = (lax.axis_index("range") * range_width + lax.iota(jnp.int32, range_width)).astype(
        jnp.float32
    ) / range_total
    for level_index in range(level_count):
        own_half = slot_index >> level_index & 1
        far_half = 1 - own_half
        extended = with_halo(images, (("range", 2),), RIM_CELLS)
        own_share = contribute(
            extended,
            ang_table[level_index, own_half, own_half],
            range_table[level_index, own_half, own_half],
            interp_taps[level_index, own_half, own_half],
            phase_twist[level_index, own_half, own_half],
            fraction,
        )
        partner_image = swapped(extended, "aperture", level_index)
        images = own_share + contribute(
            partner_image,
            ang_table[level_index, own_half, far_half],
            range_table[level_index, own_half, far_half],
            interp_taps[level_index, own_half, far_half],
            phase_twist[level_index, own_half, far_half],
            fraction,
        )
    return images[None]


LANES = 128
SUBS = 8
STEP = 16
SPAN = 2 * RIM_CELLS
NEAR = 2 * INTERP_LEN
FAR = NEAR + 2 * STEP


def table_kernel(*refs, total):
    given, outs, local = refs[:6], refs[6:13], refs[13:19]
    line, sems = refs[19:]
    copies = [pltpu.make_async_copy(a, b, sems.at[i]) for i, (a, b) in enumerate(zip(given, local))]
    for copy in copies:
        copy.start()
    core, slot, column = (lax.axis_index(a) for a in ("range", "aperture", "beam"))
    for copy in copies:
        copy.wait()
    chirp, phase, ang, offset, taps, twist = local
    (near_mat, edge_mat, steer), outs = outs[:3], outs[3:]
    line[...] = jnp.zeros_like(line)
    line[:2, : chirp.shape[1]] = chirp[...].astype(jnp.float32)
    bins = total // 2
    pulses = phase.shape[0] // 2
    beams = phase.shape[1]
    shape = (LANES, 2 * LANES)
    t_r, t_i = (
        pltpu.roll(jnp.broadcast_to(line[i : i + 1, :], shape), 0, 1, stride=1, stride_axis=0)
        for i in (0, 1)
    )
    for matrix, rows, cols in ((near_mat, LANES, 2 * LANES), (edge_mat, SPAN, LANES)):
        real, imag = t_r[:rows, :cols].astype(jnp.bfloat16), t_i[:rows, :cols].astype(jnp.bfloat16)
        matrix[:rows, :cols] = real
        matrix[:rows, cols:] = imag
        matrix[rows:, :cols] = -imag
        matrix[rows:, cols:] = real
    scale = phase.shape[0] ** (-0.5)
    for x in (0, 1):
        half = column ^ x
        angle = phase[pl.ds(pl.multiple_of(half * pulses, pulses), pulses), :]
        cos_part = (jnp.cos(angle) * scale).astype(jnp.bfloat16)
        sin_part = (-jnp.sin(angle) * scale).astype(jnp.bfloat16)
        low, high = x * pulses, (x + 1) * pulses
        steer[low:high, :beams] = cos_part
        steer[low:high, beams:] = sin_part
        steer[2 * pulses + low : 2 * pulses + high, :beams] = -sin_part
        steer[2 * pulses + low : 2 * pulses + high, beams:] = cos_part
    sub = lax.broadcasted_iota(jnp.int32, (SUBS, LANES), 0)

    def rows(line):
        return jnp.where((sub & 1) == 0, line[:, :LANES], line[:, LANES:])

    sign = jnp.where(sub < SUBS // 2, 1.0, -1.0)
    ang_out, shift_out = outs[0], outs[1]
    todo = []
    for level in (0, 1):
        table = outs[2 + level]
        own = (slot >> level) & 1
        for order in (0, 1):
            child = own if order == 0 else 1 - own
            ang_out[level, order] = ang[level, own, pl.ds(child, 1), :]
            shift_out[level, order] = rows(offset[level, own, pl.ds(child, 1), :]) + (
                RIM_CELLS - INTERP_LEN // 2 + 1
            )
            for t in range(INTERP_LEN):
                table[order, t] = rows(taps[level, own, child, 0, t : t + 1, :])
                table[order, INTERP_LEN + t] = sign * rows(taps[level, own, child, 1, t : t + 1, :])
            rate = sign * rows(twist[level, own, pl.ds(child, 1), :])
            half_bins = (bins + SPAN) // 2 if level == 0 else bins // 2
            first = core * bins + ((sub >> 1) & 1) * half_bins
            first = first - RIM_CELLS if level == 0 else first
            todo.append((table, order, rate, first, half_bins // STEP))

    for table, order, rate, first, steps in todo:
        power = 1
        near, far = {0: (jnp.ones_like(rate), jnp.zeros_like(rate))}, {0: phasor(rate, first, total)}
        while power < STEP:
            turn = phasor(rate, power, total)
            near.update({n + power: product(near[n], turn) for n in list(near)})
            power *= 2
        count = 1
        while count < steps:
            turn = phasor(rate, count * STEP, total)
            far.update({n + count: product(far[n], turn) for n in list(far) if n + count < steps})
            count *= 2
        for found, place, length in ((near, NEAR, STEP), (far, FAR, steps)):
            for n in range(length):
                table[order, place + n], table[order, place + length + n] = found[n]


def phasor(rate, count, total):
    angle = rate * (jnp.asarray(count, jnp.float32) / total)
    return jnp.cos(angle), jnp.sin(angle)


def product(x, y):
    return x[0] * y[0] - x[1] * y[1], x[0] * y[1] + x[1] * y[0]


def squeeze(piece, rim, core, near_mat, edge_mat, c_ref):
    bins = piece.shape[-1]

    def columns(low, high):
        found = []
        for ri in (0, 1):
            tiles = []
            for tile in range(low, high):
                if tile == 0:
                    other = rim[ri]
                    tiles.append(jnp.where(core == 1, other, jnp.zeros_like(other)))
                elif tile == bins // LANES + 1:
                    other = rim[ri]
                    tiles.append(jnp.where(core == 0, other, jnp.zeros_like(other)))
                else:
                    tiles.append(piece[ri, :, (tile - 1) * LANES : tile * LANES])
            found += tiles
        return jnp.concatenate(found, axis=1)

    def times(matrix, cols):
        return lax.dot_general(
            matrix, cols, (((1,), (1,)), ((), ())), preferred_element_type=jnp.float32
        )

    for block in range(bins // LANES + 2):
        if block == 0:
            rows = jnp.concatenate([near_mat[LANES - SPAN : LANES], near_mat[2 * LANES - SPAN :]], 0)
            result = times(rows, columns(0, 2))
            result = jnp.where(core == 1, result, 0.0).astype(jnp.bfloat16)
            place, count = 0, SPAN
        elif block <= bins // LANES:
            result = times(near_mat[...], columns(block, block + 2)).astype(jnp.bfloat16)
            place, count = SPAN + (block - 1) * LANES, LANES
        else:
            result = times(edge_mat[...], columns(block, block + 1)).astype(jnp.bfloat16)
            place, count = SPAN + bins, SPAN
        c_ref[0, place : place + count] = result[:count]
        c_ref[1, place : place + count] = result[count:]


def form(halves, steer, x_ref):
    pieces = [half[ri] for ri in (0, 1) for half in halves]
    image = jnp.dot(
        jnp.concatenate(pieces, axis=1), steer[...], preferred_element_type=jnp.float32
    ).astype(jnp.bfloat16)
    beams = x_ref.shape[2]
    x_ref[0] = image[:, :beams]
    x_ref[1] = image[:, beams:]


def merge_child(x_ref, ang, shift, table, s_ref, y_ref, base_ref, o_ref, half_bins):
    beams = x_ref.shape[2]
    beam_index = lax.broadcasted_iota(jnp.int32, (beams, beams), 0)
    hits = jnp.where(beam_index == ang[...], 1.0, 0.0).astype(jnp.bfloat16)
    length = half_bins + SPAN
    for ri in (0, 1):
        picked = jnp.dot(x_ref[ri], hits, preferred_element_type=jnp.float32)
        for half in (0, 1):
            for part in (0, 1):
                s_ref[pl.ds(ri * 4 + half * 2 + part, length, stride=SUBS), :] = picked[
                    half * half_bins : half * half_bins + length, part * LANES : (part + 1) * LANES
                ]
    offset = shift[...]
    bits = [(offset & (1 << b)) != 0 for b in range(5)]
    steps = half_bins // STEP
    for step in range(steps + 1):
        base = step * STEP
        row = [s_ref[pl.ds((base + k) * SUBS, SUBS), :] for k in range(STEP + 31)]
        for b in (4, 3, 2, 1, 0):
            d = 1 << b
            row = [jnp.where(bits[b], row[k + d], row[k]) for k in range(len(row) - d)]
        for k in range(STEP):
            y_ref[pl.ds((base + k) * SUBS, SUBS), :] = row[k]
    taps = INTERP_LEN
    for step in range(steps):
        far_r, far_i = table[FAR + step], table[FAR + steps + step]
        w_r, w_i = [], []
        for t in range(taps):
            a, b = table[t], table[taps + t]
            w_r.append(a * far_r - b * far_i)
            w_i.append(a * far_i + b * far_r)
        for low in range(0, STEP, SUBS):
            base = step * STEP + low
            row = [y_ref[pl.ds((base + k) * SUBS, SUBS), :] for k in range(SUBS + taps - 1)]
            for k in range(SUBS):
                a, b = row[k] * w_r[0], row[k] * w_i[0]
                for t in range(1, taps):
                    a = a + row[k + t] * w_r[t]
                    b = b + row[k + t] * w_i[t]
                e_r, e_i = table[NEAR + low + k], table[NEAR + STEP + low + k]
                value = (e_r * a - e_i * b) + pltpu.roll(e_i * a + e_r * b, SUBS // 2, 0)
                place = pl.ds((base + k) * SUBS, SUBS)
                o_ref[place, :] = value if base_ref is None else base_ref[place, :] + value


def merged_image(o_ref, x_ref, half_bins, first_bin, total):
    for half in (0, 1):
        bin_index = lax.broadcasted_iota(jnp.int32, (half_bins, 2 * LANES), 0)
        bin_index = bin_index + (first_bin + half * half_bins)
        inside = (bin_index >= 0) & (bin_index < total)
        for ri in (0, 1):
            value = jnp.concatenate(
                [
                    o_ref[pl.ds(ri * 4 + half * 2 + part, half_bins, stride=SUBS), :]
                    for part in (0, 1)
                ],
                axis=1,
            )
            x_ref[ri, half * half_bins : (half + 1) * half_bins] = jnp.where(
                inside, value, 0.0
            ).astype(jnp.bfloat16)


def finished(o_ref, out_ref, half_bins):
    for ri in (0, 1):
        for half in (0, 1):
            for part in (0, 1):
                value = o_ref[pl.ds(ri * 4 + half * 2 + part, half_bins, stride=SUBS), :]
                out_ref[
                    0, ri, part * LANES : (part + 1) * LANES, half * half_bins : (half + 1) * half_bins
                ] = value.T


def merge_low(halves, order, shared, table0, x0_ref, s_ref, y_ref, base, out_ref, half_bins):
    near_mat, edge_mat, steer, ang, shift = shared
    form(halves, steer, x0_ref)
    merge_child(
        x0_ref, ang.at[0, order], shift.at[0, order], table0.at[order], s_ref, y_ref, base, out_ref, half_bins
    )


def merge_top(o_ref, order, shared, table1, x1_ref, s_ref, y_ref, base, out_ref, half_bins, total):
    near_mat, edge_mat, steer, ang, shift = shared
    first = lax.axis_index("range") * (total // 2) - RIM_CELLS
    merged_image(o_ref, x1_ref, x1_ref.shape[1] // 2, first, total)
    merge_child(
        x1_ref, ang.at[1, order], shift.at[1, order], table1.at[order], s_ref, y_ref, base, out_ref, half_bins
    )


def first_stage(total, *refs):
    pieces, shared, table0, refs = refs[:8], refs[8:13], refs[13], refs[14:]
    part, c_own, c_next, c_a, c_b, x0_ref, s_ref, y_ref = refs
    core = lax.axis_index("range")
    for i, c_ref in enumerate((c_a, c_b, c_own, c_next)):
        squeeze(pieces[2 * i], pieces[2 * i + 1], core, shared[0], shared[1], c_ref)
    half0 = part.shape[0] // (SUBS)
    merge_low((c_a, c_b), 1, shared, table0, x0_ref, s_ref, y_ref, None, part, half0)


def second_stage(total, *refs):
    pieces, shared, table0, refs = refs[:4], refs[4:9], refs[9], refs[10:]
    table1, part, c_own = refs[:3]
    near, c_b, c_a, x0_ref, s_ref, y_ref, o_ref, x1_ref = refs[3:]
    core = lax.axis_index("range")
    for i, c_ref in enumerate((c_a, c_b)):
        squeeze(pieces[2 * i], pieces[2 * i + 1], core, shared[0], shared[1], c_ref)
    half0, half1 = o_ref.shape[0] // SUBS, near.shape[0] // SUBS
    merge_low((c_own, c_a), 0, shared, table0, x0_ref, s_ref, y_ref, part, o_ref, half0)
    merge_top(o_ref, 0, shared, table1, x1_ref, s_ref, y_ref, None, near, half1, total)


def third_stage(total, *refs):
    pieces, shared, table0, refs = refs[:2], refs[2:7], refs[7], refs[8:]
    c_next, c_b = refs[:2]
    other, c_last, x0_ref, s_ref, y_ref = refs[2:]
    core = lax.axis_index("range")
    squeeze(pieces[0], pieces[1], core, shared[0], shared[1], c_last)
    half0 = other.shape[0] // SUBS
    merge_low((c_next, c_b), 0, shared, table0, x0_ref, s_ref, y_ref, None, other, half0)


def last_stage(total, *refs):
    pieces, shared, table0, refs = refs[:2], refs[2:7], refs[7], refs[8:]
    table1, near, other, c_last = refs[:4]
    out_ref, c_a, x0_ref, s_ref, y_ref, o_ref, x1_ref, final = refs[4:]
    core = lax.axis_index("range")
    squeeze(pieces[0], pieces[1], core, shared[0], shared[1], c_a)
    half0, half1 = o_ref.shape[0] // SUBS, final.shape[0] // SUBS
    merge_low((c_last, c_a), 1, shared, table0, x0_ref, s_ref, y_ref, other, o_ref, half0)
    merge_top(o_ref, 1, shared, table1, x1_ref, s_ref, y_ref, near, final, half1, total)
    finished(final, out_ref, half1)


def ring_of_chips(echoes, chirp_taps, steer_phase, ang_table, range_table, interp_taps, phase_twist):
    pulses, bins = echoes.shape[1:]
    beams = steer_phase.shape[1]
    total = bins * lax.axis_size("range")
    slots = lax.axis_size("aperture")
    slot, column = lax.axis_index("aperture"), lax.axis_index("beam")
    axes = ("aperture", "beam")
    order = [z * 2 for z in range(slots)] + [z * 2 + 1 for z in reversed(range(slots))]
    ahead = [(order[i], order[(i + 1) % len(order)]) for i in range(len(order))]
    behind = [(b, a) for a, b in ahead]
    kind = jnp.where(column == 0, slot, slots - 1 - slot)
    half0, half1 = (bins + SPAN) // 2, bins // 2
    window = bins + 2 * SPAN

    core = lax.axis_index("range")

    def other_core(x):
        rim = jnp.where(core == 0, x[:, :, bins - LANES :], x[:, :, :LANES])
        return lax.ppermute(rim, "range", [(0, 1), (1, 0)])

    def choose(*options):
        picked = options[-1]
        for value, option in enumerate(options[:-1]):
            if option is not picked:
                picked = jnp.where(kind == value, option, picked)
        return picked

    vmem = pl.BlockSpec(memory_space=pltpu.VMEM)
    f32, bf16, i32 = jnp.float32, jnp.bfloat16, jnp.int32
    rows0 = NEAR + 2 * STEP + 2 * (half0 // STEP)
    rows1 = NEAR + 2 * STEP + 2 * (half1 // STEP)
    arguments = (chirp_taps, steer_phase, ang_table, range_table, interp_taps, phase_twist)
    tables = pl.pallas_call(
        functools.partial(table_kernel, total=total),
        out_shape=[
            jax.ShapeDtypeStruct((2 * LANES, 4 * LANES), bf16),
            jax.ShapeDtypeStruct((2 * SPAN, 2 * LANES), bf16),
            jax.ShapeDtypeStruct((4 * pulses, 2 * beams), bf16),
            jax.ShapeDtypeStruct((2, 2, 1, beams), i32),
            jax.ShapeDtypeStruct((2, 2, SUBS, LANES), i32),
            jax.ShapeDtypeStruct((2, rows0, SUBS, LANES), f32),
            jax.ShapeDtypeStruct((2, rows1, SUBS, LANES), f32),
        ],
        in_specs=[pl.BlockSpec(memory_space=pltpu.HBM)] * 6,
        out_specs=[vmem] * 7,
        scratch_shapes=[
            *(pltpu.VMEM(x.shape, x.dtype) for x in arguments),
            pltpu.VMEM((SUBS, 2 * LANES), f32),
            pltpu.SemaphoreType.DMA((len(arguments),)),
        ],
        compiler_params=pltpu.CompilerParams(vmem_limit_bytes=60 * 2**20),
        cost_estimate=pl.CostEstimate(flops=10**9, bytes_accessed=4 * 2**20, transcendentals=0),
        name="tables",
    )(*arguments)
    shared, table0, table1 = tables[:5], tables[5], tables[6]

    rows = (half0 + SPAN + 32) * SUBS
    squeezed = ((2, window, pulses), bf16)
    sums0, sums1 = ((half0 * SUBS, LANES), f32), ((half1 * SUBS, LANES), f32)
    image0, image1 = ((2, window, beams), bf16), ((2, window - SPAN, beams), bf16)
    room = ((rows, LANES), f32)

    def run(kernel, pieces, carried, out, scratch):
        given = [x for piece in pieces for x in piece] + [*shared, table0, *carried]
        return pl.pallas_call(
            functools.partial(kernel, total),
            out_shape=[jax.ShapeDtypeStruct(*x) for x in out],
            in_specs=[vmem] * len(given),
            out_specs=[vmem] * len(out),
            scratch_shapes=[pltpu.VMEM(*x) for x in scratch],
            compiler_params=pltpu.CompilerParams(vmem_limit_bytes=24 * 1024 * 1024),
            cost_estimate=pl.CostEstimate(
                flops=3 * 10**9, bytes_accessed=4 * 2**20, transcendentals=0
            ),
            name=kernel.__name__,
        )(*given)

    def after(value, result):
        return lax.optimization_barrier((value, result))[0]

    def pair(x):
        return (x, other_core(x))

    up1, down1 = lax.ppermute(echoes, axes, ahead), lax.ppermute(echoes, axes, behind)
    own = pair(echoes)
    up1, down1 = after(up1, shared[0]), after(down1, shared[0])
    up2, down2 = lax.ppermute(up1, axes, ahead), lax.ppermute(down1, axes, behind)
    beside = pair(choose(down1, up1, down1, up1))
    up3, down3 = lax.ppermute(up2, axes, ahead), lax.ppermute(down2, axes, behind)
    part, c_own, c_next = run(
        first_stage,
        [
            beside,
            pair(choose(up2, up2, down2, down2)),
            own,
            pair(choose(down2, down2, up2, up2)),
        ],
        [],
        [sums0, squeezed, squeezed],
        [squeezed, squeezed, image0, room, room],
    )
    up3, down3 = after(up3, part), after(down3, part)
    far_up, far_down = lax.ppermute(up3[:1], axes, ahead), lax.ppermute(down3[1:], axes, behind)
    last = pair(choose(down3, down1, up1, up3))
    near, c_b = run(
        second_stage,
        [pair(choose(up1, up3, down3, down1)), pair(choose(up3, down3, up3, down3))],
        [table1, part, c_own],
        [sums1, squeezed],
        [squeezed, image0, room, room, sums0, image1],
    )
    far = pair(jnp.concatenate([after(far_up, near), after(far_down, near)], axis=0))
    other, c_last = run(
        third_stage, [last], [c_next, c_b], [sums0, squeezed], [image0, room, room]
    )
    return run(
        last_stage,
        [(far[0], after(far[1], other))],
        [table1, near, other, c_last],
        [((1, 2, beams, bins), f32)],
        [squeezed, image0, room, room, sums0, image1, sums1],
    )[0]


def solution(mesh):
    small = (mesh.shape["aperture"], mesh.shape["beam"], mesh.shape["range"]) == (4, 2, 2)
    return jax.shard_map(
        ring_of_chips if small else level_by_level,
        mesh=mesh,
        in_specs=(
            P(None, ("groups", "aperture", "beam"), "range"),
            P(),
            P(None, "beam"),
            P(None, None, None, "beam"),
            P(None, None, None, "beam"),
            P(None, None, None, None, None, "beam"),
            P(None, None, None, "beam"),
        ),
        out_specs=P(("groups", "aperture"), None, "beam", "range"),
        check_vma=False,
    )
```

```python
import functools

import jax
import jax.numpy as jnp
from jax import lax
from jax.experimental import pallas as pl
from jax.experimental.pallas import tpu as pltpu
from jax.sharding import PartitionSpec as P

INTERP_LEN = 8
RIM_CELLS = 16


def from_behind(value, axis, steps):
    count = lax.axis_size(axis)
    leading, last = (max(0, -steps), min(count, count - steps))
    return lax.ppermute(value, axis, [(source, source + steps) for source in range(leading, last)])


def with_halo(x, sides, width):
    for axis, dim in sides:
        peers, length = (lax.axis_size(axis), x.shape[dim])
        up = [(i, (i + 1) % peers) for i in range(peers - 1)]
        down = [(j, i) for i, j in up]
        last = lax.slice_in_dim(x, length - width, length, axis=dim)
        leading = lax.slice_in_dim(x, 0, width, axis=dim)
        before = lax.ppermute(last, axis, up)
        after = lax.ppermute(leading, axis, down)
        x = jnp.concatenate([before, x, after], axis=dim)
    return x


def swapped(value, axis, stride):
    mask = 2**stride
    pairs = [(source, source ^ mask) for source in range(lax.axis_size(axis))]
    return lax.ppermute(value, axis, pairs)


def transposed_dot(left_side, right_side):
    return lax.dot_general(
        left_side, right_side, (((0,), (0,)), ((), ())), preferred_element_type=jnp.float32
    )


def toeplitz_matrix(chirp_taps):
    tap_count = chirp_taps.shape[1]
    row_index = lax.broadcasted_iota(jnp.int32, (128 + tap_count, 128), 0)
    col_index = lax.broadcasted_iota(jnp.int32, (128 + tap_count, 128), 1)
    lag_index = row_index - col_index
    tap_index = lax.iota(jnp.int32, tap_count)
    tap_hits = (lag_index[:, :, None] == tap_index[None, None, :]).astype(jnp.float32)
    real_part = jnp.sum(tap_hits * chirp_taps[0].astype(jnp.float32), axis=2)
    imag_part = jnp.sum(tap_hits * chirp_taps[1].astype(jnp.float32), axis=2)
    upper_half = jnp.concatenate([real_part, -imag_part], axis=1)
    lower_half = jnp.concatenate([imag_part, real_part], axis=1)
    return jnp.concatenate([upper_half, lower_half], axis=0).astype(jnp.bfloat16)


def compress(main_cols, upper_rim, kernel):
    piece_rows = main_cols.shape[1]
    range_width = main_cols.shape[2]
    tap_count = upper_rim.shape[2]
    blocks = range_width // 128
    filler = jnp.zeros((2, piece_rows, 128 - tap_count), main_cols.dtype)
    padded = jnp.concatenate([main_cols, upper_rim, filler], axis=2)
    head_cols = padded[:, :, :range_width].reshape(2, piece_rows, blocks, 128)
    tail_cols = padded[:, :, 128 : range_width + 128].reshape(2, piece_rows, blocks, 128)[
        :, :, :, :tap_count
    ]
    windows = jnp.concatenate([head_cols, tail_cols], axis=3)
    row_blocks = jnp.transpose(windows, (1, 2, 0, 3)).reshape(
        piece_rows * blocks, 2 * (128 + tap_count)
    )
    result = jnp.dot(row_blocks, kernel, preferred_element_type=jnp.float32)
    result = result.reshape(piece_rows, blocks, 2, 128)
    return (
        jnp.transpose(result, (2, 0, 1, 3)).reshape(2, piece_rows, range_width).astype(jnp.bfloat16)
    )


def contribute(extended, angles, offsets, weights, rates, fraction):
    range_width = fraction.shape[0]
    span = 2 * RIM_CELLS + 1
    picked = jnp.take(extended, angles, axis=1)
    shift_list = lax.iota(jnp.int32, span) - RIM_CELLS
    tap_list = lax.iota(jnp.int32, INTERP_LEN)
    lag_table = offsets[None, :] + tap_list[:, None] - (INTERP_LEN // 2 - 1)
    hits = (lag_table[None, :, :] == shift_list[:, None, None]).astype(jnp.float32)
    spread_real = jnp.sum(hits * weights[0][None, :, :], axis=1)
    spread_imag = jnp.sum(hits * weights[1][None, :, :], axis=1)
    real_part = jnp.zeros((angles.shape[0], range_width), jnp.float32)
    imag_part = jnp.zeros((angles.shape[0], range_width), jnp.float32)
    for shift_index in range(span):
        tap_real = spread_real[shift_index][:, None]
        tap_imag = spread_imag[shift_index][:, None]
        part_real = picked[0, :, shift_index : shift_index + range_width]
        part_imag = picked[1, :, shift_index : shift_index + range_width]
        real_part = real_part + tap_real * part_real - tap_imag * part_imag
        imag_part = imag_part + tap_real * part_imag + tap_imag * part_real
    rot_angle = rates[:, None] * fraction[None, :]
    cosine = jnp.cos(rot_angle)
    sine_value = jnp.sin(rot_angle)
    return jnp.stack(
        [real_part * cosine - imag_part * sine_value, real_part * sine_value + imag_part * cosine]
    )


def level_by_level(echoes, chirp_taps, steer_phase, ang_table, range_table, interp_taps, phase_twist):
    tap_count = chirp_taps.shape[1]
    kernel = toeplitz_matrix(chirp_taps)
    upper_rim = from_behind(echoes[:, :, :tap_count], "range", -1)
    sub_rows = steer_phase.shape[0]
    range_width = echoes.shape[2]
    steer_scale = sub_rows ** (-0.5)
    cos_table = (jnp.cos(steer_phase) * steer_scale).astype(jnp.bfloat16)
    sin_table = (-jnp.sin(steer_phase) * steer_scale).astype(jnp.bfloat16)
    compressed = compress(echoes, upper_rim, kernel)
    shard_rows = lax.all_gather(compressed, "beam", axis=1, tiled=True)
    real_part = transposed_dot(cos_table, shard_rows[0]) - transposed_dot(sin_table, shard_rows[1])
    imag_part = transposed_dot(cos_table, shard_rows[1]) + transposed_dot(sin_table, shard_rows[0])
    images = jnp.stack([real_part, imag_part])
    slot_index = lax.axis_index("aperture")
    level_count = lax.axis_size("aperture").bit_length() - 1
    range_total = range_width * lax.axis_size("range")
    fraction = (lax.axis_index("range") * range_width + lax.iota(jnp.int32, range_width)).astype(
        jnp.float32
    ) / range_total
    for level_index in range(level_count):
        own_half = slot_index >> level_index & 1
        far_half = 1 - own_half
        extended = with_halo(images, (("range", 2),), RIM_CELLS)
        own_share = contribute(
            extended,
            ang_table[level_index, own_half, own_half],
            range_table[level_index, own_half, own_half],
            interp_taps[level_index, own_half, own_half],
            phase_twist[level_index, own_half, own_half],
            fraction,
        )
        partner_image = swapped(extended, "aperture", level_index)
        images = own_share + contribute(
            partner_image,
            ang_table[level_index, own_half, far_half],
            range_table[level_index, own_half, far_half],
            interp_taps[level_index, own_half, far_half],
            phase_twist[level_index, own_half, far_half],
            fraction,
        )
    return images[None]


LANES = 128
SUBS = 8
STEP = 16
SPAN = 2 * RIM_CELLS
NEAR = 2 * INTERP_LEN
FAR = NEAR + 2 * STEP


def table_kernel(*refs, total):
    given, outs, local = refs[:6], refs[6:13], refs[13:19]
    line, sems = refs[19:]
    copies = [pltpu.make_async_copy(a, b, sems.at[i]) for i, (a, b) in enumerate(zip(given, local))]
    for copy in copies:
        copy.start()
    core, slot, column = (lax.axis_index(a) for a in ("range", "aperture", "beam"))
    for copy in copies:
        copy.wait()
    chirp, phase, ang, offset, taps, twist = local
    (near_mat, edge_mat, steer), outs = outs[:3], outs[3:]
    line[...] = jnp.zeros_like(line)
    line[:2, : chirp.shape[1]] = chirp[...].astype(jnp.float32)
    bins = total // 2
    pulses = phase.shape[0] // 2
    beams = phase.shape[1]
    shape = (LANES, 2 * LANES)
    t_r, t_i = (
        pltpu.roll(jnp.broadcast_to(line[i : i + 1, :], shape), 0, 1, stride=1, stride_axis=0)
        for i in (0, 1)
    )
    for matrix, rows, cols in ((near_mat, LANES, 2 * LANES), (edge_mat, SPAN, LANES)):
        real, imag = t_r[:rows, :cols].astype(jnp.bfloat16), t_i[:rows, :cols].astype(jnp.bfloat16)
        matrix[:rows, :cols] = real
        matrix[:rows, cols:] = imag
        matrix[rows:, :cols] = -imag
        matrix[rows:, cols:] = real
    scale = phase.shape[0] ** (-0.5)
    for x in (0, 1):
        half = column ^ x
        angle = phase[pl.ds(pl.multiple_of(half * pulses, pulses), pulses), :]
        cos_part = (jnp.cos(angle) * scale).astype(jnp.bfloat16)
        sin_part = (-jnp.sin(angle) * scale).astype(jnp.bfloat16)
        low, high = x * pulses, (x + 1) * pulses
        steer[low:high, :beams] = cos_part
        steer[low:high, beams:] = sin_part
        steer[2 * pulses + low : 2 * pulses + high, :beams] = -sin_part
        steer[2 * pulses + low : 2 * pulses + high, beams:] = cos_part
    sub = lax.broadcasted_iota(jnp.int32, (SUBS, LANES), 0)

    def rows(line):
        return jnp.where((sub & 1) == 0, line[:, :LANES], line[:, LANES:])

    sign = jnp.where(sub < SUBS // 2, 1.0, -1.0)
    ang_out, shift_out = outs[0], outs[1]
    todo = []
    for level in (0, 1):
        table = outs[2 + level]
        own = (slot >> level) & 1
        for order in (0, 1):
            child = own if order == 0 else 1 - own
            ang_out[level, order] = ang[level, own, pl.ds(child, 1), :]
            shift_out[level, order] = rows(offset[level, own, pl.ds(child, 1), :]) + (
                RIM_CELLS - INTERP_LEN // 2 + 1
            )
            for t in range(INTERP_LEN):
                table[order, t] = rows(taps[level, own, child, 0, t : t + 1, :])
                table[order, INTERP_LEN + t] = sign * rows(taps[level, own, child, 1, t : t + 1, :])
            rate = sign * rows(twist[level, own, pl.ds(child, 1), :])
            half_bins = (bins + SPAN) // 2 if level == 0 else bins // 2
            first = core * bins + ((sub >> 1) & 1) * half_bins
            first = first - RIM_CELLS if level == 0 else first
            todo.append((table, order, rate, first, half_bins // STEP))

    for table, order, rate, first, steps in todo:
        power = 1
        near, far = {0: (jnp.ones_like(rate), jnp.zeros_like(rate))}, {0: phasor(rate, first, total)}
        while power < STEP:
            turn = phasor(rate, power, total)
            near.update({n + power: product(near[n], turn) for n in list(near)})
            power *= 2
        count = 1
        while count < steps:
            turn = phasor(rate, count * STEP, total)
            far.update({n + count: product(far[n], turn) for n in list(far) if n + count < steps})
            count *= 2
        for found, place, length in ((near, NEAR, STEP), (far, FAR, steps)):
            for n in range(length):
                table[order, place + n], table[order, place + length + n] = found[n]


def phasor(rate, count, total):
    angle = rate * (jnp.asarray(count, jnp.float32) / total)
    return jnp.cos(angle), jnp.sin(angle)


def product(x, y):
    return x[0] * y[0] - x[1] * y[1], x[0] * y[1] + x[1] * y[0]


def squeeze(piece, rim, core, near_mat, edge_mat, c_ref):
    bins = piece.shape[-1]

    def columns(low, high):
        found = []
        for ri in (0, 1):
            tiles = []
            for tile in range(low, high):
                if tile == 0:
                    other = rim[ri]
                    tiles.append(jnp.where(core == 1, other, jnp.zeros_like(other)))
                elif tile == bins // LANES + 1:
                    other = rim[ri]
                    tiles.append(jnp.where(core == 0, other, jnp.zeros_like(other)))
                else:
                    tiles.append(piece[ri, :, (tile - 1) * LANES : tile * LANES])
            found += tiles
        return jnp.concatenate(found, axis=1)

    def times(matrix, cols):
        return lax.dot_general(
            matrix, cols, (((1,), (1,)), ((), ())), preferred_element_type=jnp.float32
        )

    for block in range(bins // LANES + 2):
        if block == 0:
            rows = jnp.concatenate([near_mat[LANES - SPAN : LANES], near_mat[2 * LANES - SPAN :]], 0)
            result = times(rows, columns(0, 2))
            result = jnp.where(core == 1, result, 0.0).astype(jnp.bfloat16)
            place, count = 0, SPAN
        elif block <= bins // LANES:
            result = times(near_mat[...], columns(block, block + 2)).astype(jnp.bfloat16)
            place, count = SPAN + (block - 1) * LANES, LANES
        else:
            result = times(edge_mat[...], columns(block, block + 1)).astype(jnp.bfloat16)
            place, count = SPAN + bins, SPAN
        c_ref[0, place : place + count] = result[:count]
        c_ref[1, place : place + count] = result[count:]


def form(halves, steer, x_ref):
    pieces = [half[ri] for ri in (0, 1) for half in halves]
    image = jnp.dot(
        jnp.concatenate(pieces, axis=1), steer[...], preferred_element_type=jnp.float32
    ).astype(jnp.bfloat16)
    beams = x_ref.shape[2]
    x_ref[0] = image[:, :beams]
    x_ref[1] = image[:, beams:]


def merge_child(x_ref, ang, shift, table, s_ref, y_ref, z_ref, base_ref, o_ref, half_bins):
    beams = x_ref.shape[2]
    beam_index = lax.broadcasted_iota(jnp.int32, (beams, beams), 0)
    hits = jnp.where(beam_index == ang[...], 1.0, 0.0).astype(jnp.bfloat16)
    length = half_bins + SPAN
    for ri in (0, 1):
        picked = jnp.dot(x_ref[ri], hits, preferred_element_type=jnp.float32)
        for half in (0, 1):
            for part in (0, 1):
                s_ref[pl.ds(ri * 4 + half * 2 + part, length, stride=SUBS), :] = picked[
                    half * half_bins : half * half_bins + length, part * LANES : (part + 1) * LANES
                ]
    offset = shift[...]
    bits = [(offset & (1 << b)) != 0 for b in range(5)]
    taps, middle = INTERP_LEN, SUBS // 2
    n = STEP // 2
    width = n + taps - 1
    steps = half_bins // STEP
    last = half_bins + taps - 1
    for start in range(0, last, 2 * STEP):
        count = min(2 * STEP, last - start)
        row = [s_ref[pl.ds((start + k) * SUBS, SUBS), :] for k in range(count + 31)]
        for b in (4, 3, 2, 1, 0):
            d = 1 << b
            row = [jnp.where(bits[b], row[k + d], row[k]) for k in range(len(row) - d)]
        for k in range(count):
            y_ref[pl.ds((start + k) * SUBS, SUBS), :] = row[k]
            both = row[k] + pltpu.roll(row[k], middle, 0)
            for group in range(2 * steps):
                index = start + k - group * n
                if 0 <= index < width:
                    place, side = (group // 2) * width + index, (group % 2) * middle
                    z_ref[pl.ds(place * SUBS + side, middle), :] = both[side : side + middle]
    first_part = lax.broadcasted_iota(jnp.int32, (SUBS, LANES), 0) < middle

    def filtered(ref, start, weights):
        total = ref[pl.ds(start * SUBS, SUBS), :] * weights[0]
        for t in range(1, taps):
            total = total + ref[pl.ds((start + t) * SUBS, SUBS), :] * weights[t]
        return total

    for step in range(steps):
        far = table[FAR + step], table[FAR + steps + step]
        turned_taps = [product((table[t], table[taps + t]), far) for t in range(taps)]
        w_sum = [real for real, imag in turned_taps]
        w_one = [imag - real for real, imag in turned_taps]
        for k in range(n):
            shared = filtered(z_ref, step * width + k, w_sum)
            turned = pltpu.roll(shared, middle, 0)
            for low, sums in (
                (k, jnp.where(first_part, shared, turned)),
                (n + k, jnp.where(first_part, turned, shared)),
            ):
                bin_index = step * STEP + low
                value = sums + pltpu.roll(filtered(y_ref, bin_index, w_one), middle, 0)
                e_r, e_i = table[NEAR + low], table[NEAR + STEP + low]
                value = value * e_r + pltpu.roll(value * e_i, middle, 0)
                place = pl.ds(bin_index * SUBS, SUBS)
                o_ref[place, :] = value if base_ref is None else base_ref[place, :] + value


def merged_image(o_ref, x_ref, half_bins, first_bin, total):
    for half in (0, 1):
        bin_index = lax.broadcasted_iota(jnp.int32, (half_bins, 2 * LANES), 0)
        bin_index = bin_index + (first_bin + half * half_bins)
        inside = (bin_index >= 0) & (bin_index < total)
        for ri in (0, 1):
            value = jnp.concatenate(
                [
                    o_ref[pl.ds(ri * 4 + half * 2 + part, half_bins, stride=SUBS), :]
                    for part in (0, 1)
                ],
                axis=1,
            )
            x_ref[ri, half * half_bins : (half + 1) * half_bins] = jnp.where(
                inside, value, 0.0
            ).astype(jnp.bfloat16)


def finished(o_ref, out_ref, half_bins):
    for ri in (0, 1):
        for half in (0, 1):
            for part in (0, 1):
                value = o_ref[pl.ds(ri * 4 + half * 2 + part, half_bins, stride=SUBS), :]
                out_ref[
                    0, ri, part * LANES : (part + 1) * LANES, half * half_bins : (half + 1) * half_bins
                ] = value.T


def merge_low(halves, order, shared, table0, x0_ref, rooms, base, out_ref, half_bins):
    near_mat, edge_mat, steer, ang, shift = shared
    form(halves, steer, x0_ref)
    merge_child(
        x0_ref, ang.at[0, order], shift.at[0, order], table0.at[order], *rooms, base, out_ref, half_bins
    )


def merge_top(o_ref, order, shared, table1, x1_ref, rooms, base, out_ref, half_bins, total):
    near_mat, edge_mat, steer, ang, shift = shared
    first = lax.axis_index("range") * (total // 2) - RIM_CELLS
    merged_image(o_ref, x1_ref, x1_ref.shape[1] // 2, first, total)
    merge_child(
        x1_ref, ang.at[1, order], shift.at[1, order], table1.at[order], *rooms, base, out_ref, half_bins
    )


def first_stage(total, *refs):
    pieces, shared, table0, refs = refs[:8], refs[8:13], refs[13], refs[14:]
    part, c_own, c_next, c_a, c_b, x0_ref, *rooms = refs
    core = lax.axis_index("range")
    for i, c_ref in enumerate((c_a, c_b, c_own, c_next)):
        squeeze(pieces[2 * i], pieces[2 * i + 1], core, shared[0], shared[1], c_ref)
    half0 = part.shape[0] // (SUBS)
    merge_low((c_a, c_b), 1, shared, table0, x0_ref, rooms, None, part, half0)


def second_stage(total, *refs):
    pieces, shared, table0, refs = refs[:4], refs[4:9], refs[9], refs[10:]
    table1, part, c_own = refs[:3]
    near, c_b, c_a, x0_ref, o_ref, x1_ref, *rooms = refs[3:]
    core = lax.axis_index("range")
    for i, c_ref in enumerate((c_a, c_b)):
        squeeze(pieces[2 * i], pieces[2 * i + 1], core, shared[0], shared[1], c_ref)
    half0, half1 = o_ref.shape[0] // SUBS, near.shape[0] // SUBS
    merge_low((c_own, c_a), 0, shared, table0, x0_ref, rooms, part, o_ref, half0)
    merge_top(o_ref, 0, shared, table1, x1_ref, rooms, None, near, half1, total)


def third_stage(total, *refs):
    pieces, shared, table0, refs = refs[:2], refs[2:7], refs[7], refs[8:]
    c_next, c_b = refs[:2]
    other, c_last, x0_ref, *rooms = refs[2:]
    core = lax.axis_index("range")
    squeeze(pieces[0], pieces[1], core, shared[0], shared[1], c_last)
    half0 = other.shape[0] // SUBS
    merge_low((c_next, c_b), 0, shared, table0, x0_ref, rooms, None, other, half0)


def last_stage(total, *refs):
    pieces, shared, table0, refs = refs[:2], refs[2:7], refs[7], refs[8:]
    table1, near, other, c_last = refs[:4]
    out_ref, c_a, x0_ref, o_ref, x1_ref, final, *rooms = refs[4:]
    core = lax.axis_index("range")
    squeeze(pieces[0], pieces[1], core, shared[0], shared[1], c_a)
    half0, half1 = o_ref.shape[0] // SUBS, final.shape[0] // SUBS
    merge_low((c_last, c_a), 1, shared, table0, x0_ref, rooms, other, o_ref, half0)
    merge_top(o_ref, 1, shared, table1, x1_ref, rooms, near, final, half1, total)
    finished(final, out_ref, half1)


def ring_of_chips(echoes, chirp_taps, steer_phase, ang_table, range_table, interp_taps, phase_twist):
    pulses, bins = echoes.shape[1:]
    beams = steer_phase.shape[1]
    total = bins * lax.axis_size("range")
    slots = lax.axis_size("aperture")
    slot, column = lax.axis_index("aperture"), lax.axis_index("beam")
    axes = ("aperture", "beam")
    order = [z * 2 for z in range(slots)] + [z * 2 + 1 for z in reversed(range(slots))]
    ahead = [(order[i], order[(i + 1) % len(order)]) for i in range(len(order))]
    behind = [(b, a) for a, b in ahead]
    kind = jnp.where(column == 0, slot, slots - 1 - slot)
    half0, half1 = (bins + SPAN) // 2, bins // 2
    window = bins + 2 * SPAN

    core = lax.axis_index("range")

    def other_core(x):
        rim = jnp.where(core == 0, x[:, :, bins - LANES :], x[:, :, :LANES])
        return lax.ppermute(rim, "range", [(0, 1), (1, 0)])

    def choose(*options):
        picked = options[-1]
        for value, option in enumerate(options[:-1]):
            if option is not picked:
                picked = jnp.where(kind == value, option, picked)
        return picked

    vmem = pl.BlockSpec(memory_space=pltpu.VMEM)
    f32, bf16, i32 = jnp.float32, jnp.bfloat16, jnp.int32
    rows0 = NEAR + 2 * STEP + 2 * (half0 // STEP)
    rows1 = NEAR + 2 * STEP + 2 * (half1 // STEP)
    arguments = (chirp_taps, steer_phase, ang_table, range_table, interp_taps, phase_twist)
    tables = pl.pallas_call(
        functools.partial(table_kernel, total=total),
        out_shape=[
            jax.ShapeDtypeStruct((2 * LANES, 4 * LANES), bf16),
            jax.ShapeDtypeStruct((2 * SPAN, 2 * LANES), bf16),
            jax.ShapeDtypeStruct((4 * pulses, 2 * beams), bf16),
            jax.ShapeDtypeStruct((2, 2, 1, beams), i32),
            jax.ShapeDtypeStruct((2, 2, SUBS, LANES), i32),
            jax.ShapeDtypeStruct((2, rows0, SUBS, LANES), f32),
            jax.ShapeDtypeStruct((2, rows1, SUBS, LANES), f32),
        ],
        in_specs=[pl.BlockSpec(memory_space=pltpu.HBM)] * 6,
        out_specs=[vmem] * 7,
        scratch_shapes=[
            *(pltpu.VMEM(x.shape, x.dtype) for x in arguments),
            pltpu.VMEM((SUBS, 2 * LANES), f32),
            pltpu.SemaphoreType.DMA((len(arguments),)),
        ],
        compiler_params=pltpu.CompilerParams(vmem_limit_bytes=60 * 2**20),
        cost_estimate=pl.CostEstimate(flops=10**9, bytes_accessed=4 * 2**20, transcendentals=0),
        name="tables",
    )(*arguments)
    shared, table0, table1 = tables[:5], tables[5], tables[6]

    rows = (half0 + SPAN + 32) * SUBS
    squeezed = ((2, window, pulses), bf16)
    sums0, sums1 = ((half0 * SUBS, LANES), f32), ((half1 * SUBS, LANES), f32)
    image0, image1 = ((2, window, beams), bf16), ((2, window - SPAN, beams), bf16)
    rooms = [((rows, LANES), f32)] * 3

    def run(kernel, pieces, carried, out, scratch):
        given = [x for piece in pieces for x in piece] + [*shared, table0, *carried]
        return pl.pallas_call(
            functools.partial(kernel, total),
            out_shape=[jax.ShapeDtypeStruct(*x) for x in out],
            in_specs=[vmem] * len(given),
            out_specs=[vmem] * len(out),
            scratch_shapes=[pltpu.VMEM(*x) for x in scratch],
            compiler_params=pltpu.CompilerParams(vmem_limit_bytes=24 * 1024 * 1024),
            cost_estimate=pl.CostEstimate(
                flops=3 * 10**9, bytes_accessed=4 * 2**20, transcendentals=0
            ),
            name=kernel.__name__,
        )(*given)

    def after(value, result):
        return lax.optimization_barrier((value, result))[0]

    def pair(x):
        return (x, other_core(x))

    up1, down1 = lax.ppermute(echoes, axes, ahead), lax.ppermute(echoes, axes, behind)
    own = pair(echoes)
    up1, down1 = after(up1, shared[0]), after(down1, shared[0])
    up2, down2 = lax.ppermute(up1, axes, ahead), lax.ppermute(down1, axes, behind)
    beside = pair(choose(down1, up1, down1, up1))
    up3, down3 = lax.ppermute(up2, axes, ahead), lax.ppermute(down2, axes, behind)
    part, c_own, c_next = run(
        first_stage,
        [
            beside,
            pair(choose(up2, up2, down2, down2)),
            own,
            pair(choose(down2, down2, up2, up2)),
        ],
        [],
        [sums0, squeezed, squeezed],
        [squeezed, squeezed, image0, *rooms],
    )
    up3, down3 = after(up3, part), after(down3, part)
    far_up, far_down = lax.ppermute(up3[:1], axes, ahead), lax.ppermute(down3[1:], axes, behind)
    last = pair(choose(down3, down1, up1, up3))
    near, c_b = run(
        second_stage,
        [pair(choose(up1, up3, down3, down1)), pair(choose(up3, down3, up3, down3))],
        [table1, part, c_own],
        [sums1, squeezed],
        [squeezed, image0, sums0, image1, *rooms],
    )
    far = pair(jnp.concatenate([after(far_up, near), after(far_down, near)], axis=0))
    other, c_last = run(
        third_stage, [last], [c_next, c_b], [sums0, squeezed], [image0, *rooms]
    )
    return run(
        last_stage,
        [(far[0], after(far[1], other))],
        [table1, near, other, c_last],
        [((1, 2, beams, bins), f32)],
        [squeezed, image0, sums0, image1, sums1, *rooms],
    )[0]


def solution(mesh):
    small = (mesh.shape["aperture"], mesh.shape["beam"], mesh.shape["range"]) == (4, 2, 2)
    return jax.shard_map(
        ring_of_chips if small else level_by_level,
        mesh=mesh,
        in_specs=(
            P(None, ("groups", "aperture", "beam"), "range"),
            P(),
            P(None, "beam"),
            P(None, None, None, "beam"),
            P(None, None, None, "beam"),
            P(None, None, None, None, None, "beam"),
            P(None, None, None, "beam"),
        ),
        out_specs=P(("groups", "aperture"), None, "beam", "range"),
        check_vma=False,
    )
```

```python
import functools

import jax
import jax.numpy as jnp
from jax import lax
from jax.experimental import pallas as pl
from jax.experimental.pallas import tpu as pltpu
from jax.sharding import PartitionSpec as P

INTERP_LEN = 8
RIM_CELLS = 16


def from_behind(value, axis, steps):
    count = lax.axis_size(axis)
    leading, last = (max(0, -steps), min(count, count - steps))
    return lax.ppermute(value, axis, [(source, source + steps) for source in range(leading, last)])


def with_halo(x, sides, width):
    for axis, dim in sides:
        peers, length = (lax.axis_size(axis), x.shape[dim])
        up = [(i, (i + 1) % peers) for i in range(peers - 1)]
        down = [(j, i) for i, j in up]
        last = lax.slice_in_dim(x, length - width, length, axis=dim)
        leading = lax.slice_in_dim(x, 0, width, axis=dim)
        before = lax.ppermute(last, axis, up)
        after = lax.ppermute(leading, axis, down)
        x = jnp.concatenate([before, x, after], axis=dim)
    return x


def swapped(value, axis, stride):
    mask = 2**stride
    pairs = [(source, source ^ mask) for source in range(lax.axis_size(axis))]
    return lax.ppermute(value, axis, pairs)


def transposed_dot(left_side, right_side):
    return lax.dot_general(
        left_side, right_side, (((0,), (0,)), ((), ())), preferred_element_type=jnp.float32
    )


def toeplitz_matrix(chirp_taps):
    tap_count = chirp_taps.shape[1]
    row_index = lax.broadcasted_iota(jnp.int32, (128 + tap_count, 128), 0)
    col_index = lax.broadcasted_iota(jnp.int32, (128 + tap_count, 128), 1)
    lag_index = row_index - col_index
    tap_index = lax.iota(jnp.int32, tap_count)
    tap_hits = (lag_index[:, :, None] == tap_index[None, None, :]).astype(jnp.float32)
    real_part = jnp.sum(tap_hits * chirp_taps[0].astype(jnp.float32), axis=2)
    imag_part = jnp.sum(tap_hits * chirp_taps[1].astype(jnp.float32), axis=2)
    upper_half = jnp.concatenate([real_part, -imag_part], axis=1)
    lower_half = jnp.concatenate([imag_part, real_part], axis=1)
    return jnp.concatenate([upper_half, lower_half], axis=0).astype(jnp.bfloat16)


def compress(main_cols, upper_rim, kernel):
    piece_rows = main_cols.shape[1]
    range_width = main_cols.shape[2]
    tap_count = upper_rim.shape[2]
    blocks = range_width // 128
    filler = jnp.zeros((2, piece_rows, 128 - tap_count), main_cols.dtype)
    padded = jnp.concatenate([main_cols, upper_rim, filler], axis=2)
    head_cols = padded[:, :, :range_width].reshape(2, piece_rows, blocks, 128)
    tail_cols = padded[:, :, 128 : range_width + 128].reshape(2, piece_rows, blocks, 128)[
        :, :, :, :tap_count
    ]
    windows = jnp.concatenate([head_cols, tail_cols], axis=3)
    row_blocks = jnp.transpose(windows, (1, 2, 0, 3)).reshape(
        piece_rows * blocks, 2 * (128 + tap_count)
    )
    result = jnp.dot(row_blocks, kernel, preferred_element_type=jnp.float32)
    result = result.reshape(piece_rows, blocks, 2, 128)
    return (
        jnp.transpose(result, (2, 0, 1, 3)).reshape(2, piece_rows, range_width).astype(jnp.bfloat16)
    )


def contribute(extended, angles, offsets, weights, rates, fraction):
    range_width = fraction.shape[0]
    span = 2 * RIM_CELLS + 1
    picked = jnp.take(extended, angles, axis=1)
    shift_list = lax.iota(jnp.int32, span) - RIM_CELLS
    tap_list = lax.iota(jnp.int32, INTERP_LEN)
    lag_table = offsets[None, :] + tap_list[:, None] - (INTERP_LEN // 2 - 1)
    hits = (lag_table[None, :, :] == shift_list[:, None, None]).astype(jnp.float32)
    spread_real = jnp.sum(hits * weights[0][None, :, :], axis=1)
    spread_imag = jnp.sum(hits * weights[1][None, :, :], axis=1)
    real_part = jnp.zeros((angles.shape[0], range_width), jnp.float32)
    imag_part = jnp.zeros((angles.shape[0], range_width), jnp.float32)
    for shift_index in range(span):
        tap_real = spread_real[shift_index][:, None]
        tap_imag = spread_imag[shift_index][:, None]
        part_real = picked[0, :, shift_index : shift_index + range_width]
        part_imag = picked[1, :, shift_index : shift_index + range_width]
        real_part = real_part + tap_real * part_real - tap_imag * part_imag
        imag_part = imag_part + tap_real * part_imag + tap_imag * part_real
    rot_angle = rates[:, None] * fraction[None, :]
    cosine = jnp.cos(rot_angle)
    sine_value = jnp.sin(rot_angle)
    return jnp.stack(
        [real_part * cosine - imag_part * sine_value, real_part * sine_value + imag_part * cosine]
    )


def level_by_level(echoes, chirp_taps, steer_phase, ang_table, range_table, interp_taps, phase_twist):
    tap_count = chirp_taps.shape[1]
    kernel = toeplitz_matrix(chirp_taps)
    upper_rim = from_behind(echoes[:, :, :tap_count], "range", -1)
    sub_rows = steer_phase.shape[0]
    range_width = echoes.shape[2]
    steer_scale = sub_rows ** (-0.5)
    cos_table = (jnp.cos(steer_phase) * steer_scale).astype(jnp.bfloat16)
    sin_table = (-jnp.sin(steer_phase) * steer_scale).astype(jnp.bfloat16)
    compressed = compress(echoes, upper_rim, kernel)
    shard_rows = lax.all_gather(compressed, "beam", axis=1, tiled=True)
    real_part = transposed_dot(cos_table, shard_rows[0]) - transposed_dot(sin_table, shard_rows[1])
    imag_part = transposed_dot(cos_table, shard_rows[1]) + transposed_dot(sin_table, shard_rows[0])
    images = jnp.stack([real_part, imag_part])
    slot_index = lax.axis_index("aperture")
    level_count = lax.axis_size("aperture").bit_length() - 1
    range_total = range_width * lax.axis_size("range")
    fraction = (lax.axis_index("range") * range_width + lax.iota(jnp.int32, range_width)).astype(
        jnp.float32
    ) / range_total
    for level_index in range(level_count):
        own_half = slot_index >> level_index & 1
        far_half = 1 - own_half
        extended = with_halo(images, (("range", 2),), RIM_CELLS)
        own_share = contribute(
            extended,
            ang_table[level_index, own_half, own_half],
            range_table[level_index, own_half, own_half],
            interp_taps[level_index, own_half, own_half],
            phase_twist[level_index, own_half, own_half],
            fraction,
        )
        partner_image = swapped(extended, "aperture", level_index)
        images = own_share + contribute(
            partner_image,
            ang_table[level_index, own_half, far_half],
            range_table[level_index, own_half, far_half],
            interp_taps[level_index, own_half, far_half],
            phase_twist[level_index, own_half, far_half],
            fraction,
        )
    return images[None]


LANES = 128
SUBS = 8
STEP = 16
SPAN = 2 * RIM_CELLS
NEAR = 2 * INTERP_LEN
FAR = NEAR + 2 * STEP


def table_kernel(*refs, total):
    given, outs, local = refs[:6], refs[6:13], refs[13:19]
    line, sems = refs[19:]
    copies = [pltpu.make_async_copy(a, b, sems.at[i]) for i, (a, b) in enumerate(zip(given, local))]
    for copy in copies:
        copy.start()
    core, slot, column = (lax.axis_index(a) for a in ("range", "aperture", "beam"))
    for copy in copies:
        copy.wait()
    chirp, phase, ang, offset, taps, twist = local
    (near_mat, edge_mat, steer), outs = outs[:3], outs[3:]
    line[...] = jnp.zeros_like(line)
    line[:2, : chirp.shape[1]] = chirp[...].astype(jnp.float32)
    bins = total // 2
    pulses = phase.shape[0] // 2
    beams = phase.shape[1]
    shape = (LANES, 2 * LANES)
    t_r, t_i = (
        pltpu.roll(jnp.broadcast_to(line[i : i + 1, :], shape), 0, 1, stride=1, stride_axis=0)
        for i in (0, 1)
    )
    for matrix, rows, cols in ((near_mat, LANES, 2 * LANES), (edge_mat, SPAN, LANES)):
        real, imag = t_r[:rows, :cols].astype(jnp.bfloat16), t_i[:rows, :cols].astype(jnp.bfloat16)
        matrix[:rows, :cols] = real
        matrix[:rows, cols:] = imag
        matrix[rows:, :cols] = -imag
        matrix[rows:, cols:] = real
    scale = phase.shape[0] ** (-0.5)
    for x in (0, 1):
        half = column ^ x
        angle = phase[pl.ds(pl.multiple_of(half * pulses, pulses), pulses), :]
        cos_part = (jnp.cos(angle) * scale).astype(jnp.bfloat16)
        sin_part = (-jnp.sin(angle) * scale).astype(jnp.bfloat16)
        low, high = x * pulses, (x + 1) * pulses
        steer[low:high, :beams] = cos_part
        steer[low:high, beams:] = sin_part
        steer[2 * pulses + low : 2 * pulses + high, :beams] = -sin_part
        steer[2 * pulses + low : 2 * pulses + high, beams:] = cos_part
    sub = lax.broadcasted_iota(jnp.int32, (SUBS, LANES), 0)

    def rows(line):
        return jnp.where((sub & 1) == 0, line[:, :LANES], line[:, LANES:])

    sign = jnp.where(sub < SUBS // 2, 1.0, -1.0)
    ang_out, shift_out = outs[0], outs[1]
    todo = []
    for level in (0, 1):
        table = outs[2 + level]
        own = (slot >> level) & 1
        for order in (0, 1):
            child = own if order == 0 else 1 - own
            ang_out[level, order] = ang[level, own, pl.ds(child, 1), :]
            shift_out[level, order] = rows(offset[level, own, pl.ds(child, 1), :]) + (
                RIM_CELLS - INTERP_LEN // 2 + 1
            )
            for t in range(INTERP_LEN):
                table[order, t] = rows(taps[level, own, child, 0, t : t + 1, :])
                table[order, INTERP_LEN + t] = sign * rows(taps[level, own, child, 1, t : t + 1, :])
            rate = sign * rows(twist[level, own, pl.ds(child, 1), :])
            half_bins = (bins + SPAN) // 2 if level == 0 else bins // 2
            first = core * bins + ((sub >> 1) & 1) * half_bins
            first = first - RIM_CELLS if level == 0 else first
            todo.append((table, order, rate, first, half_bins // STEP))

    for table, order, rate, first, steps in todo:
        power = 1
        near, far = {0: (jnp.ones_like(rate), jnp.zeros_like(rate))}, {0: phasor(rate, first, total)}
        while power < STEP:
            turn = phasor(rate, power, total)
            near.update({n + power: product(near[n], turn) for n in list(near)})
            power *= 2
        count = 1
        while count < steps:
            turn = phasor(rate, count * STEP, total)
            far.update({n + count: product(far[n], turn) for n in list(far) if n + count < steps})
            count *= 2
        for found, place, length in ((near, NEAR, STEP), (far, FAR, steps)):
            for n in range(length):
                table[order, place + n], table[order, place + length + n] = found[n]


def phasor(rate, count, total):
    angle = rate * (jnp.asarray(count, jnp.float32) / total)
    return jnp.cos(angle), jnp.sin(angle)


def product(x, y):
    return x[0] * y[0] - x[1] * y[1], x[0] * y[1] + x[1] * y[0]


def squeeze(piece, rim, core, near_mat, edge_mat, c_ref):
    bins = piece.shape[-1]

    def columns(low, high):
        found = []
        for ri in (0, 1):
            tiles = []
            for tile in range(low, high):
                if tile == 0:
                    other = rim[ri]
                    tiles.append(jnp.where(core == 1, other, jnp.zeros_like(other)))
                elif tile == bins // LANES + 1:
                    other = rim[ri]
                    tiles.append(jnp.where(core == 0, other, jnp.zeros_like(other)))
                else:
                    tiles.append(piece[ri, :, (tile - 1) * LANES : tile * LANES])
            found += tiles
        return jnp.concatenate(found, axis=1)

    def times(matrix, cols):
        return lax.dot_general(
            matrix, cols, (((1,), (1,)), ((), ())), preferred_element_type=jnp.float32
        )

    for block in range(bins // LANES + 2):
        if block == 0:
            rows = jnp.concatenate([near_mat[LANES - SPAN : LANES], near_mat[2 * LANES - SPAN :]], 0)
            result = times(rows, columns(0, 2))
            result = jnp.where(core == 1, result, 0.0).astype(jnp.bfloat16)
            place, count = 0, SPAN
        elif block <= bins // LANES:
            result = times(near_mat[...], columns(block, block + 2)).astype(jnp.bfloat16)
            place, count = SPAN + (block - 1) * LANES, LANES
        else:
            result = times(edge_mat[...], columns(block, block + 1)).astype(jnp.bfloat16)
            place, count = SPAN + bins, SPAN
        c_ref[0, place : place + count] = result[:count]
        c_ref[1, place : place + count] = result[count:]


def form(halves, steer, x_ref):
    pieces = [
        jnp.where(half[0], half[1][ri], half[2][ri]) if isinstance(half, tuple) else half[ri]
        for ri in (0, 1)
        for half in halves
    ]
    image = jnp.dot(
        jnp.concatenate(pieces, axis=1), steer[...], preferred_element_type=jnp.float32
    ).astype(jnp.bfloat16)
    beams = x_ref.shape[2]
    x_ref[0] = image[:, :beams]
    x_ref[1] = image[:, beams:]


def merge_child(x_ref, ang, shift, table, s_ref, y_ref, z_ref, base_ref, o_ref, half_bins):
    beams = x_ref.shape[2]
    beam_index = lax.broadcasted_iota(jnp.int32, (beams, beams), 0)
    hits = jnp.where(beam_index == ang[...], 1.0, 0.0).astype(jnp.bfloat16)
    length = half_bins + SPAN
    for ri in (0, 1):
        picked = jnp.dot(x_ref[ri], hits, preferred_element_type=jnp.float32)
        for half in (0, 1):
            for part in (0, 1):
                s_ref[pl.ds(ri * 4 + half * 2 + part, length, stride=SUBS), :] = picked[
                    half * half_bins : half * half_bins + length, part * LANES : (part + 1) * LANES
                ]
    offset = shift[...]
    bits = [(offset & (1 << b)) != 0 for b in range(5)]
    taps, middle = INTERP_LEN, SUBS // 2
    n = STEP // 2
    width = n + taps - 1
    steps = half_bins // STEP
    last = half_bins + taps - 1
    for start in range(0, last, 2 * STEP):
        count = min(2 * STEP, last - start)
        row = [s_ref[pl.ds((start + k) * SUBS, SUBS), :] for k in range(count + 31)]
        for b in (4, 3, 2, 1, 0):
            d = 1 << b
            row = [jnp.where(bits[b], row[k + d], row[k]) for k in range(len(row) - d)]
        for k in range(count):
            y_ref[pl.ds((start + k) * SUBS, SUBS), :] = row[k]
            both = row[k] + pltpu.roll(row[k], middle, 0)
            for group in range(2 * steps):
                index = start + k - group * n
                if 0 <= index < width:
                    place, side = (group // 2) * width + index, (group % 2) * middle
                    z_ref[pl.ds(place * SUBS + side, middle), :] = both[side : side + middle]
    first_part = lax.broadcasted_iota(jnp.int32, (SUBS, LANES), 0) < middle

    def filtered(ref, start, weights):
        total = ref[pl.ds(start * SUBS, SUBS), :] * weights[0]
        for t in range(1, taps):
            total = total + ref[pl.ds((start + t) * SUBS, SUBS), :] * weights[t]
        return total

    for step in range(steps):
        far = table[FAR + step], table[FAR + steps + step]
        turned_taps = [product((table[t], table[taps + t]), far) for t in range(taps)]
        w_sum = [real for real, imag in turned_taps]
        w_one = [imag - real for real, imag in turned_taps]
        for k in range(n):
            shared = filtered(z_ref, step * width + k, w_sum)
            turned = pltpu.roll(shared, middle, 0)
            for low, sums in (
                (k, jnp.where(first_part, shared, turned)),
                (n + k, jnp.where(first_part, turned, shared)),
            ):
                bin_index = step * STEP + low
                value = sums + pltpu.roll(filtered(y_ref, bin_index, w_one), middle, 0)
                e_r, e_i = table[NEAR + low], table[NEAR + STEP + low]
                value = value * e_r + pltpu.roll(value * e_i, middle, 0)
                place = pl.ds(bin_index * SUBS, SUBS)
                o_ref[place, :] = value if base_ref is None else base_ref[place, :] + value


def merged_image(o_ref, x_ref, half_bins, first_bin, total):
    for half in (0, 1):
        bin_index = lax.broadcasted_iota(jnp.int32, (half_bins, 2 * LANES), 0)
        bin_index = bin_index + (first_bin + half * half_bins)
        inside = (bin_index >= 0) & (bin_index < total)
        for ri in (0, 1):
            value = jnp.concatenate(
                [
                    o_ref[pl.ds(ri * 4 + half * 2 + part, half_bins, stride=SUBS), :]
                    for part in (0, 1)
                ],
                axis=1,
            )
            x_ref[ri, half * half_bins : (half + 1) * half_bins] = jnp.where(
                inside, value, 0.0
            ).astype(jnp.bfloat16)


def finished(o_ref, image, out_ref, sems, half_bins):
    copies = []
    for ri in (0, 1):
        for part in (0, 1):
            beams = pl.ds(part * LANES, LANES)
            for half in (0, 1):
                value = o_ref[pl.ds(ri * 4 + half * 2 + part, half_bins, stride=SUBS), :]
                image[ri, beams, half * half_bins : (half + 1) * half_bins] = value.T
            copies.append(
                pltpu.make_async_copy(
                    image.at[ri, beams], out_ref.at[0, ri, beams], sems.at[len(copies)]
                )
            )
            copies[-1].start()
    for copy in copies:
        copy.wait()


def merge_low(halves, order, shared, table0, x0_ref, rooms, base, out_ref, half_bins):
    near_mat, edge_mat, steer, ang, shift = shared
    form(halves, steer, x0_ref)
    merge_child(
        x0_ref, ang.at[0, order], shift.at[0, order], table0.at[order], *rooms, base, out_ref, half_bins
    )


def merge_top(o_ref, order, shared, table1, x1_ref, rooms, base, out_ref, half_bins, total):
    near_mat, edge_mat, steer, ang, shift = shared
    first = lax.axis_index("range") * (total // 2) - RIM_CELLS
    merged_image(o_ref, x1_ref, x1_ref.shape[1] // 2, first, total)
    merge_child(
        x1_ref, ang.at[1, order], shift.at[1, order], table1.at[order], *rooms, base, out_ref, half_bins
    )


def outer():
    slot = lax.axis_index("aperture")
    return (slot == 0) | (slot == lax.axis_size("aperture") - 1)


def first_stage(total, *refs):
    pieces, shared, table0, refs = refs[:10], refs[10:15], refs[15], refs[16:]
    part, c_own, c_next, c_early, c_a, c_b, x0_ref, *rooms = refs
    core = lax.axis_index("range")
    for i, c_ref in enumerate((c_a, c_b, c_own, c_next, c_early)):
        squeeze(pieces[2 * i], pieces[2 * i + 1], core, shared[0], shared[1], c_ref)
    half0 = part.shape[0] // (SUBS)
    merge_low((c_a, c_b), 1, shared, table0, x0_ref, rooms, None, part, half0)


def second_stage(total, *refs):
    pieces, shared, table0, refs = refs[:4], refs[4:9], refs[9], refs[10:]
    table1, part, c_own, c_early = refs[:4]
    near, c_b, c_late, x0_ref, o_ref, x1_ref, *rooms = refs[4:]
    core = lax.axis_index("range")
    for i, c_ref in enumerate((c_late, c_b)):
        squeeze(pieces[2 * i], pieces[2 * i + 1], core, shared[0], shared[1], c_ref)
    half0, half1 = o_ref.shape[0] // SUBS, near.shape[0] // SUBS
    second = (outer(), c_early, c_late)
    merge_low((c_own, second), 0, shared, table0, x0_ref, rooms, part, o_ref, half0)
    merge_top(o_ref, 0, shared, table1, x1_ref, rooms, None, near, half1, total)


def third_stage(total, *refs):
    shared, table0, c_next, c_b = refs[:5], refs[5], refs[6], refs[7]
    other, x0_ref, *rooms = refs[8:]
    half0 = other.shape[0] // SUBS
    merge_low((c_next, c_b), 0, shared, table0, x0_ref, rooms, None, other, half0)


def last_stage(total, *refs):
    pieces, shared, table0, refs = refs[:2], refs[2:7], refs[7], refs[8:]
    table1, near, other, c_early, c_late = refs[:5]
    out_ref, c_a, x0_ref, o_ref, x1_ref, final, image, sems, *rooms = refs[5:]
    core = lax.axis_index("range")
    squeeze(pieces[0], pieces[1], core, shared[0], shared[1], c_a)
    half0, half1 = o_ref.shape[0] // SUBS, final.shape[0] // SUBS
    first = (outer(), c_late, c_early)
    merge_low((first, c_a), 1, shared, table0, x0_ref, rooms, other, o_ref, half0)
    merge_top(o_ref, 1, shared, table1, x1_ref, rooms, near, final, half1, total)
    finished(final, image, out_ref, sems, half1)


def ring_of_chips(echoes, chirp_taps, steer_phase, ang_table, range_table, interp_taps, phase_twist):
    pulses, bins = echoes.shape[1:]
    beams = steer_phase.shape[1]
    total = bins * lax.axis_size("range")
    slots = lax.axis_size("aperture")
    slot, column = lax.axis_index("aperture"), lax.axis_index("beam")
    axes = ("aperture", "beam")
    order = [z * 2 for z in range(slots)] + [z * 2 + 1 for z in reversed(range(slots))]
    ahead = [(order[i], order[(i + 1) % len(order)]) for i in range(len(order))]
    behind = [(b, a) for a, b in ahead]
    kind = jnp.where(column == 0, slot, slots - 1 - slot)
    half0, half1 = (bins + SPAN) // 2, bins // 2
    window = bins + 2 * SPAN

    core = lax.axis_index("range")

    def pairs(*pieces):
        rims = [jnp.where(core == 0, x[:, :, bins - LANES :], x[:, :, :LANES]) for x in pieces]
        rims = lax.ppermute(jnp.concatenate(rims, axis=0), "range", [(0, 1), (1, 0)])
        return [(x, rims[2 * i : 2 * i + 2]) for i, x in enumerate(pieces)]

    def choose(*options):
        picked = options[-1]
        for value, option in enumerate(options[:-1]):
            if option is not picked:
                picked = jnp.where(kind == value, option, picked)
        return picked

    vmem = pl.BlockSpec(memory_space=pltpu.VMEM)
    f32, bf16, i32 = jnp.float32, jnp.bfloat16, jnp.int32
    rows0 = NEAR + 2 * STEP + 2 * (half0 // STEP)
    rows1 = NEAR + 2 * STEP + 2 * (half1 // STEP)
    arguments = (chirp_taps, steer_phase, ang_table, range_table, interp_taps, phase_twist)
    tables = pl.pallas_call(
        functools.partial(table_kernel, total=total),
        out_shape=[
            jax.ShapeDtypeStruct((2 * LANES, 4 * LANES), bf16),
            jax.ShapeDtypeStruct((2 * SPAN, 2 * LANES), bf16),
            jax.ShapeDtypeStruct((4 * pulses, 2 * beams), bf16),
            jax.ShapeDtypeStruct((2, 2, 1, beams), i32),
            jax.ShapeDtypeStruct((2, 2, SUBS, LANES), i32),
            jax.ShapeDtypeStruct((2, rows0, SUBS, LANES), f32),
            jax.ShapeDtypeStruct((2, rows1, SUBS, LANES), f32),
        ],
        in_specs=[pl.BlockSpec(memory_space=pltpu.HBM)] * 6,
        out_specs=[vmem] * 7,
        scratch_shapes=[
            *(pltpu.VMEM(x.shape, x.dtype) for x in arguments),
            pltpu.VMEM((SUBS, 2 * LANES), f32),
            pltpu.SemaphoreType.DMA((len(arguments),)),
        ],
        compiler_params=pltpu.CompilerParams(vmem_limit_bytes=60 * 2**20),
        cost_estimate=pl.CostEstimate(flops=10**9, bytes_accessed=4 * 2**20, transcendentals=0),
        name="tables",
    )(*arguments)
    shared, table0, table1 = tables[:5], tables[5], tables[6]

    rows = (half0 + SPAN + 32) * SUBS
    squeezed = ((2, window, pulses), bf16)
    sums0, sums1 = ((half0 * SUBS, LANES), f32), ((half1 * SUBS, LANES), f32)
    image0, image1 = ((2, window, beams), bf16), ((2, window - SPAN, beams), bf16)
    rooms = [((rows, LANES), f32)] * 3

    def run(kernel, pieces, carried, out, scratch, place=vmem):
        given = [x for piece in pieces for x in piece] + [*shared, table0, *carried]
        return pl.pallas_call(
            functools.partial(kernel, total),
            out_shape=[jax.ShapeDtypeStruct(*x) for x in out],
            in_specs=[vmem] * len(given),
            out_specs=[place] * len(out),
            scratch_shapes=[pltpu.VMEM(*x) if isinstance(x, tuple) else x for x in scratch],
            compiler_params=pltpu.CompilerParams(vmem_limit_bytes=24 * 1024 * 1024),
            cost_estimate=pl.CostEstimate(
                flops=3 * 10**9, bytes_accessed=4 * 2**20, transcendentals=0
            ),
            name=kernel.__name__,
        )(*given)

    def after(value, result):
        return lax.optimization_barrier((value, result))[0]

    up1, down1 = lax.ppermute(echoes, axes, ahead), lax.ppermute(echoes, axes, behind)
    own = pairs(echoes)
    up1, down1 = after(up1, shared[0]), after(down1, shared[0])
    up2, down2 = lax.ppermute(up1, axes, ahead), lax.ppermute(down1, axes, behind)
    ready = pairs(choose(down1, up1, down1, up1), choose(up1, down1, up1, down1))
    up3, down3 = lax.ppermute(up2, axes, ahead), lax.ppermute(down2, axes, behind)
    fresh = pairs(choose(up2, up2, down2, down2), choose(down2, down2, up2, up2))
    part, c_own, c_next, c_early = run(
        first_stage,
        [ready[0], fresh[0], *own, fresh[1], ready[1]],
        [],
        [sums0, squeezed, squeezed, squeezed],
        [squeezed, squeezed, image0, *rooms],
    )
    up3, down3 = after(up3, part), after(down3, part)
    far_up, far_down = lax.ppermute(up3[:1], axes, ahead), lax.ppermute(down3[1:], axes, behind)
    near, c_b, c_late = run(
        second_stage,
        pairs(choose(down3, up3, down3, up3), choose(up3, down3, up3, down3)),
        [table1, part, c_own, c_early],
        [sums1, squeezed, squeezed],
        [image0, sums0, image1, *rooms],
    )
    far = pairs(jnp.concatenate([after(far_up, near), after(far_down, near)], axis=0))[0]
    other = run(third_stage, [], [c_next, c_b], [sums0], [image0, *rooms])[0]
    return run(
        last_stage,
        [(far[0], after(far[1], other))],
        [table1, near, other, c_early, c_late],
        [((1, 2, beams, bins), f32)],
        [
            squeezed,
            image0,
            sums0,
            image1,
            sums1,
            ((2, beams, bins), f32),
            pltpu.SemaphoreType.DMA((4,)),
            *rooms,
        ],
        pl.BlockSpec(memory_space=pl.ANY),
    )[0]


def solution(mesh):
    small = (mesh.shape["aperture"], mesh.shape["beam"], mesh.shape["range"]) == (4, 2, 2)
    return jax.shard_map(
        ring_of_chips if small else level_by_level,
        mesh=mesh,
        in_specs=(
            P(None, ("groups", "aperture", "beam"), "range"),
            P(),
            P(None, "beam"),
            P(None, None, None, "beam"),
            P(None, None, None, "beam"),
            P(None, None, None, None, None, "beam"),
            P(None, None, None, "beam"),
        ),
        out_specs=P(("groups", "aperture"), None, "beam", "range"),
        check_vma=False,
    )
```

```python
import functools

import jax
import jax.numpy as jnp
from jax import lax
from jax.experimental import pallas as pl
from jax.experimental.pallas import tpu as pltpu
from jax.sharding import PartitionSpec as P

INTERP_LEN = 8
RIM_CELLS = 16


def from_behind(value, axis, steps):
    count = lax.axis_size(axis)
    leading, last = (max(0, -steps), min(count, count - steps))
    return lax.ppermute(value, axis, [(source, source + steps) for source in range(leading, last)])


def with_halo(x, sides, width):
    for axis, dim in sides:
        peers, length = (lax.axis_size(axis), x.shape[dim])
        up = [(i, (i + 1) % peers) for i in range(peers - 1)]
        down = [(j, i) for i, j in up]
        last = lax.slice_in_dim(x, length - width, length, axis=dim)
        leading = lax.slice_in_dim(x, 0, width, axis=dim)
        before = lax.ppermute(last, axis, up)
        after = lax.ppermute(leading, axis, down)
        x = jnp.concatenate([before, x, after], axis=dim)
    return x


def swapped(value, axis, stride):
    mask = 2**stride
    pairs = [(source, source ^ mask) for source in range(lax.axis_size(axis))]
    return lax.ppermute(value, axis, pairs)


def transposed_dot(left_side, right_side):
    return lax.dot_general(
        left_side, right_side, (((0,), (0,)), ((), ())), preferred_element_type=jnp.float32
    )


def toeplitz_matrix(chirp_taps):
    tap_count = chirp_taps.shape[1]
    row_index = lax.broadcasted_iota(jnp.int32, (128 + tap_count, 128), 0)
    col_index = lax.broadcasted_iota(jnp.int32, (128 + tap_count, 128), 1)
    lag_index = row_index - col_index
    tap_index = lax.iota(jnp.int32, tap_count)
    tap_hits = (lag_index[:, :, None] == tap_index[None, None, :]).astype(jnp.float32)
    real_part = jnp.sum(tap_hits * chirp_taps[0].astype(jnp.float32), axis=2)
    imag_part = jnp.sum(tap_hits * chirp_taps[1].astype(jnp.float32), axis=2)
    upper_half = jnp.concatenate([real_part, -imag_part], axis=1)
    lower_half = jnp.concatenate([imag_part, real_part], axis=1)
    return jnp.concatenate([upper_half, lower_half], axis=0).astype(jnp.bfloat16)


def compress(main_cols, upper_rim, kernel):
    piece_rows = main_cols.shape[1]
    range_width = main_cols.shape[2]
    tap_count = upper_rim.shape[2]
    blocks = range_width // 128
    filler = jnp.zeros((2, piece_rows, 128 - tap_count), main_cols.dtype)
    padded = jnp.concatenate([main_cols, upper_rim, filler], axis=2)
    head_cols = padded[:, :, :range_width].reshape(2, piece_rows, blocks, 128)
    tail_cols = padded[:, :, 128 : range_width + 128].reshape(2, piece_rows, blocks, 128)[
        :, :, :, :tap_count
    ]
    windows = jnp.concatenate([head_cols, tail_cols], axis=3)
    row_blocks = jnp.transpose(windows, (1, 2, 0, 3)).reshape(
        piece_rows * blocks, 2 * (128 + tap_count)
    )
    result = jnp.dot(row_blocks, kernel, preferred_element_type=jnp.float32)
    result = result.reshape(piece_rows, blocks, 2, 128)
    return (
        jnp.transpose(result, (2, 0, 1, 3)).reshape(2, piece_rows, range_width).astype(jnp.bfloat16)
    )


def contribute(extended, angles, offsets, weights, rates, fraction):
    range_width = fraction.shape[0]
    span = 2 * RIM_CELLS + 1
    picked = jnp.take(extended, angles, axis=1)
    shift_list = lax.iota(jnp.int32, span) - RIM_CELLS
    tap_list = lax.iota(jnp.int32, INTERP_LEN)
    lag_table = offsets[None, :] + tap_list[:, None] - (INTERP_LEN // 2 - 1)
    hits = (lag_table[None, :, :] == shift_list[:, None, None]).astype(jnp.float32)
    spread_real = jnp.sum(hits * weights[0][None, :, :], axis=1)
    spread_imag = jnp.sum(hits * weights[1][None, :, :], axis=1)
    real_part = jnp.zeros((angles.shape[0], range_width), jnp.float32)
    imag_part = jnp.zeros((angles.shape[0], range_width), jnp.float32)
    for shift_index in range(span):
        tap_real = spread_real[shift_index][:, None]
        tap_imag = spread_imag[shift_index][:, None]
        part_real = picked[0, :, shift_index : shift_index + range_width]
        part_imag = picked[1, :, shift_index : shift_index + range_width]
        real_part = real_part + tap_real * part_real - tap_imag * part_imag
        imag_part = imag_part + tap_real * part_imag + tap_imag * part_real
    rot_angle = rates[:, None] * fraction[None, :]
    cosine = jnp.cos(rot_angle)
    sine_value = jnp.sin(rot_angle)
    return jnp.stack(
        [real_part * cosine - imag_part * sine_value, real_part * sine_value + imag_part * cosine]
    )


def level_by_level(echoes, chirp_taps, steer_phase, ang_table, range_table, interp_taps, phase_twist):
    tap_count = chirp_taps.shape[1]
    kernel = toeplitz_matrix(chirp_taps)
    upper_rim = from_behind(echoes[:, :, :tap_count], "range", -1)
    sub_rows = steer_phase.shape[0]
    range_width = echoes.shape[2]
    steer_scale = sub_rows ** (-0.5)
    cos_table = (jnp.cos(steer_phase) * steer_scale).astype(jnp.bfloat16)
    sin_table = (-jnp.sin(steer_phase) * steer_scale).astype(jnp.bfloat16)
    compressed = compress(echoes, upper_rim, kernel)
    shard_rows = lax.all_gather(compressed, "beam", axis=1, tiled=True)
    real_part = transposed_dot(cos_table, shard_rows[0]) - transposed_dot(sin_table, shard_rows[1])
    imag_part = transposed_dot(cos_table, shard_rows[1]) + transposed_dot(sin_table, shard_rows[0])
    images = jnp.stack([real_part, imag_part])
    slot_index = lax.axis_index("aperture")
    level_count = lax.axis_size("aperture").bit_length() - 1
    range_total = range_width * lax.axis_size("range")
    fraction = (lax.axis_index("range") * range_width + lax.iota(jnp.int32, range_width)).astype(
        jnp.float32
    ) / range_total
    for level_index in range(level_count):
        own_half = slot_index >> level_index & 1
        far_half = 1 - own_half
        extended = with_halo(images, (("range", 2),), RIM_CELLS)
        own_share = contribute(
            extended,
            ang_table[level_index, own_half, own_half],
            range_table[level_index, own_half, own_half],
            interp_taps[level_index, own_half, own_half],
            phase_twist[level_index, own_half, own_half],
            fraction,
        )
        partner_image = swapped(extended, "aperture", level_index)
        images = own_share + contribute(
            partner_image,
            ang_table[level_index, own_half, far_half],
            range_table[level_index, own_half, far_half],
            interp_taps[level_index, own_half, far_half],
            phase_twist[level_index, own_half, far_half],
            fraction,
        )
    return images[None]


LANES = 128
SUBS = 8
STEP = 16
SPAN = 2 * RIM_CELLS
NEAR = 2 * INTERP_LEN
FAR = NEAR + 2 * STEP


def table_kernel(*refs, total):
    given, outs, local = refs[:6], refs[6:13], refs[13:19]
    line, sems = refs[19:]
    copies = [pltpu.make_async_copy(a, b, sems.at[i]) for i, (a, b) in enumerate(zip(given, local))]
    for copy in copies:
        copy.start()
    core, slot, column = (lax.axis_index(a) for a in ("range", "aperture", "beam"))
    for copy in copies:
        copy.wait()
    chirp, phase, ang, offset, taps, twist = local
    (near_mat, edge_mat, steer), outs = outs[:3], outs[3:]
    line[...] = jnp.zeros_like(line)
    line[:2, : chirp.shape[1]] = chirp[...].astype(jnp.float32)
    bins = total // 2
    pulses = phase.shape[0] // 2
    beams = phase.shape[1]
    shape = (LANES, 2 * LANES)
    t_r, t_i = (
        pltpu.roll(jnp.broadcast_to(line[i : i + 1, :], shape), 0, 1, stride=1, stride_axis=0)
        for i in (0, 1)
    )
    for matrix, rows, cols in ((near_mat, LANES, 2 * LANES), (edge_mat, SPAN, LANES)):
        real, imag = t_r[:rows, :cols].astype(jnp.bfloat16), t_i[:rows, :cols].astype(jnp.bfloat16)
        matrix[:rows, :cols] = real
        matrix[:rows, cols:] = imag
        matrix[rows:, :cols] = -imag
        matrix[rows:, cols:] = real
    scale = phase.shape[0] ** (-0.5)
    for x in (0, 1):
        half = column ^ x
        angle = phase[pl.ds(pl.multiple_of(half * pulses, pulses), pulses), :]
        cos_part = (jnp.cos(angle) * scale).astype(jnp.bfloat16)
        sin_part = (-jnp.sin(angle) * scale).astype(jnp.bfloat16)
        low, high = x * pulses, (x + 1) * pulses
        steer[low:high, :beams] = cos_part
        steer[low:high, beams:] = sin_part
        steer[2 * pulses + low : 2 * pulses + high, :beams] = -sin_part
        steer[2 * pulses + low : 2 * pulses + high, beams:] = cos_part
    sub = lax.broadcasted_iota(jnp.int32, (SUBS, LANES), 0)

    def rows(line):
        return jnp.where((sub & 1) == 0, line[:, :LANES], line[:, LANES:])

    sign = jnp.where(sub < SUBS // 2, 1.0, -1.0)
    ang_out, shift_out = outs[0], outs[1]
    todo = []
    for level in (0, 1):
        table = outs[2 + level]
        own = (slot >> level) & 1
        for order in (0, 1):
            child = own if order == 0 else 1 - own
            ang_out[level, order] = ang[level, own, pl.ds(child, 1), :]
            shift_out[level, order] = rows(offset[level, own, pl.ds(child, 1), :]) + (
                RIM_CELLS - INTERP_LEN // 2 + 1
            )
            for t in range(INTERP_LEN):
                table[order, t] = rows(taps[level, own, child, 0, t : t + 1, :])
                table[order, INTERP_LEN + t] = sign * rows(taps[level, own, child, 1, t : t + 1, :])
            rate = sign * rows(twist[level, own, pl.ds(child, 1), :])
            half_bins = (bins + SPAN) // 2 if level == 0 else bins // 2
            first = core * bins + ((sub >> 1) & 1) * half_bins
            first = first - RIM_CELLS if level == 0 else first
            todo.append((table, order, rate, first, half_bins // STEP))

    for table, order, rate, first, steps in todo:
        power = 1
        near, far = {0: (jnp.ones_like(rate), jnp.zeros_like(rate))}, {0: phasor(rate, first, total)}
        while power < STEP:
            turn = phasor(rate, power, total)
            near.update({n + power: product(near[n], turn) for n in list(near)})
            power *= 2
        count = 1
        while count < steps:
            turn = phasor(rate, count * STEP, total)
            far.update({n + count: product(far[n], turn) for n in list(far) if n + count < steps})
            count *= 2
        for found, place, length in ((near, NEAR, STEP), (far, FAR, steps)):
            for n in range(length):
                table[order, place + n], table[order, place + length + n] = found[n]


def phasor(rate, count, total):
    angle = rate * (jnp.asarray(count, jnp.float32) / total)
    return jnp.cos(angle), jnp.sin(angle)


def product(x, y):
    return x[0] * y[0] - x[1] * y[1], x[0] * y[1] + x[1] * y[0]


def squeeze(pieces, core, near_mat, edge_mat, c_refs):
    pulses, bins = pieces[0].shape[1:]

    def columns(low, high):
        found = []
        for ri in (0, 1):
            for tile in range(low, high):
                parts = []
                for piece, rim in zip(pieces[::2], pieces[1::2]):
                    if tile in (0, bins // LANES + 1):
                        other = rim[ri]
                        here = core == (1 if tile == 0 else 0)
                        parts.append(jnp.where(here, other, jnp.zeros_like(other)))
                    else:
                        parts.append(piece[ri, :, (tile - 1) * LANES : tile * LANES])
                found.append(jnp.concatenate(parts, axis=0))
        return jnp.concatenate(found, axis=1)

    def times(matrix, cols):
        return lax.dot_general(
            matrix, cols, (((1,), (1,)), ((), ())), preferred_element_type=jnp.float32
        )

    for block in range(bins // LANES + 2):
        if block == 0:
            rows = jnp.concatenate([near_mat[LANES - SPAN : LANES], near_mat[2 * LANES - SPAN :]], 0)
            result = times(rows, columns(0, 2))
            result = jnp.where(core == 1, result, 0.0).astype(jnp.bfloat16)
            place, count = 0, SPAN
        elif block <= bins // LANES:
            result = times(near_mat[...], columns(block, block + 2)).astype(jnp.bfloat16)
            place, count = SPAN + (block - 1) * LANES, LANES
        else:
            result = times(edge_mat[...], columns(block, block + 1)).astype(jnp.bfloat16)
            place, count = SPAN + bins, SPAN
        for i, c_ref in enumerate(c_refs):
            c_ref[0, place : place + count] = result[:count, i * pulses : (i + 1) * pulses]
            c_ref[1, place : place + count] = result[count:, i * pulses : (i + 1) * pulses]


def form(halves, steer, x_ref):
    pieces = [
        jnp.where(half[0], half[1][ri], half[2][ri]) if isinstance(half, tuple) else half[ri]
        for ri in (0, 1)
        for half in halves
    ]
    image = jnp.dot(
        jnp.concatenate(pieces, axis=1), steer[...], preferred_element_type=jnp.float32
    ).astype(jnp.bfloat16)
    beams = x_ref.shape[2]
    x_ref[0] = image[:, :beams]
    x_ref[1] = image[:, beams:]


def merge_child(x_ref, ang, shift, table, s_ref, y_ref, z_ref, base_ref, o_ref, half_bins):
    beams = x_ref.shape[2]
    beam_index = lax.broadcasted_iota(jnp.int32, (beams, beams), 0)
    hits = jnp.where(beam_index == ang[...], 1.0, 0.0).astype(jnp.bfloat16)
    length = half_bins + SPAN
    for ri in (0, 1):
        picked = jnp.dot(x_ref[ri], hits, preferred_element_type=jnp.float32)
        for half in (0, 1):
            for part in (0, 1):
                s_ref[pl.ds(ri * 4 + half * 2 + part, length, stride=SUBS), :] = picked[
                    half * half_bins : half * half_bins + length, part * LANES : (part + 1) * LANES
                ]
    offset = shift[...]
    bits = [(offset & (1 << b)) != 0 for b in range(5)]
    taps, middle = INTERP_LEN, SUBS // 2
    n = STEP // 2
    width = n + taps - 1
    steps = half_bins // STEP
    last = half_bins + taps - 1
    for start in range(0, last, 2 * STEP):
        count = min(2 * STEP, last - start)
        row = [s_ref[pl.ds((start + k) * SUBS, SUBS), :] for k in range(count + 31)]
        for b in (4, 3, 2, 1, 0):
            d = 1 << b
            row = [jnp.where(bits[b], row[k + d], row[k]) for k in range(len(row) - d)]
        for k in range(count):
            y_ref[pl.ds((start + k) * SUBS, SUBS), :] = row[k]
            both = row[k] + pltpu.roll(row[k], middle, 0)
            for group in range(2 * steps):
                index = start + k - group * n
                if 0 <= index < width:
                    place, side = (group // 2) * width + index, (group % 2) * middle
                    z_ref[pl.ds(place * SUBS + side, middle), :] = both[side : side + middle]
    first_part = lax.broadcasted_iota(jnp.int32, (SUBS, LANES), 0) < middle

    def filtered(ref, start, weights):
        total = ref[pl.ds(start * SUBS, SUBS), :] * weights[0]
        for t in range(1, taps):
            total = total + ref[pl.ds((start + t) * SUBS, SUBS), :] * weights[t]
        return total

    for step in range(steps):
        far = table[FAR + step], table[FAR + steps + step]
        turned_taps = [product((table[t], table[taps + t]), far) for t in range(taps)]
        w_sum = [real for real, imag in turned_taps]
        w_one = [imag - real for real, imag in turned_taps]
        for k in range(n):
            shared = filtered(z_ref, step * width + k, w_sum)
            turned = pltpu.roll(shared, middle, 0)
            for low, sums in (
                (k, jnp.where(first_part, shared, turned)),
                (n + k, jnp.where(first_part, turned, shared)),
            ):
                bin_index = step * STEP + low
                value = sums + pltpu.roll(filtered(y_ref, bin_index, w_one), middle, 0)
                e_r, e_i = table[NEAR + low], table[NEAR + STEP + low]
                value = value * e_r + pltpu.roll(value * e_i, middle, 0)
                place = pl.ds(bin_index * SUBS, SUBS)
                o_ref[place, :] = value if base_ref is None else base_ref[place, :] + value


def merged_image(o_ref, x_ref, half_bins, first_bin, total):
    for half in (0, 1):
        bin_index = lax.broadcasted_iota(jnp.int32, (half_bins, 2 * LANES), 0)
        bin_index = bin_index + (first_bin + half * half_bins)
        inside = (bin_index >= 0) & (bin_index < total)
        for ri in (0, 1):
            value = jnp.concatenate(
                [
                    o_ref[pl.ds(ri * 4 + half * 2 + part, half_bins, stride=SUBS), :]
                    for part in (0, 1)
                ],
                axis=1,
            )
            x_ref[ri, half * half_bins : (half + 1) * half_bins] = jnp.where(
                inside, value, 0.0
            ).astype(jnp.bfloat16)


def finished(o_ref, image, out_ref, sems, half_bins):
    copies = []
    for ri in (0, 1):
        for part in (0, 1):
            beams = pl.ds(part * LANES, LANES)
            for half in (0, 1):
                value = o_ref[pl.ds(ri * 4 + half * 2 + part, half_bins, stride=SUBS), :]
                image[ri, beams, half * half_bins : (half + 1) * half_bins] = value.T
            copies.append(
                pltpu.make_async_copy(
                    image.at[ri, beams], out_ref.at[0, ri, beams], sems.at[len(copies)]
                )
            )
            copies[-1].start()
    for copy in copies:
        copy.wait()


def merge_low(halves, order, shared, table0, x0_ref, rooms, base, out_ref, half_bins):
    near_mat, edge_mat, steer, ang, shift = shared
    form(halves, steer, x0_ref)
    merge_child(
        x0_ref, ang.at[0, order], shift.at[0, order], table0.at[order], *rooms, base, out_ref, half_bins
    )


def merge_top(o_ref, order, shared, table1, x1_ref, rooms, base, out_ref, half_bins, total):
    near_mat, edge_mat, steer, ang, shift = shared
    first = lax.axis_index("range") * (total // 2) - RIM_CELLS
    merged_image(o_ref, x1_ref, x1_ref.shape[1] // 2, first, total)
    merge_child(
        x1_ref, ang.at[1, order], shift.at[1, order], table1.at[order], *rooms, base, out_ref, half_bins
    )


def outer():
    slot = lax.axis_index("aperture")
    return (slot == 0) | (slot == lax.axis_size("aperture") - 1)


def first_stage(total, *refs):
    pieces, shared, table0, refs = refs[:10], refs[10:15], refs[15], refs[16:]
    part, c_own, c_next, c_early, c_a, c_b, x0_ref, *rooms = refs
    core = lax.axis_index("range")
    squeeze(pieces[:4], core, shared[0], shared[1], (c_a, c_b))
    squeeze(pieces[4:8], core, shared[0], shared[1], (c_own, c_next))
    squeeze(pieces[8:], core, shared[0], shared[1], (c_early,))
    half0 = part.shape[0] // (SUBS)
    merge_low((c_a, c_b), 1, shared, table0, x0_ref, rooms, None, part, half0)


def second_stage(total, *refs):
    pieces, shared, table0, refs = refs[:4], refs[4:9], refs[9], refs[10:]
    table1, part, c_own, c_early = refs[:4]
    near, c_b, c_late, x0_ref, o_ref, x1_ref, *rooms = refs[4:]
    core = lax.axis_index("range")
    squeeze(pieces, core, shared[0], shared[1], (c_late, c_b))
    half0, half1 = o_ref.shape[0] // SUBS, near.shape[0] // SUBS
    second = (outer(), c_early, c_late)
    merge_low((c_own, second), 0, shared, table0, x0_ref, rooms, part, o_ref, half0)
    merge_top(o_ref, 0, shared, table1, x1_ref, rooms, None, near, half1, total)


def third_stage(total, *refs):
    shared, table0, c_next, c_b = refs[:5], refs[5], refs[6], refs[7]
    other, x0_ref, *rooms = refs[8:]
    half0 = other.shape[0] // SUBS
    merge_low((c_next, c_b), 0, shared, table0, x0_ref, rooms, None, other, half0)


def last_stage(total, *refs):
    pieces, shared, table0, refs = refs[:2], refs[2:7], refs[7], refs[8:]
    table1, near, other, c_early, c_late = refs[:5]
    out_ref, c_a, x0_ref, o_ref, x1_ref, final, image, sems, *rooms = refs[5:]
    core = lax.axis_index("range")
    squeeze(pieces, core, shared[0], shared[1], (c_a,))
    half0, half1 = o_ref.shape[0] // SUBS, final.shape[0] // SUBS
    first = (outer(), c_late, c_early)
    merge_low((first, c_a), 1, shared, table0, x0_ref, rooms, other, o_ref, half0)
    merge_top(o_ref, 1, shared, table1, x1_ref, rooms, near, final, half1, total)
    finished(final, image, out_ref, sems, half1)


def ring_of_chips(echoes, chirp_taps, steer_phase, ang_table, range_table, interp_taps, phase_twist):
    pulses, bins = echoes.shape[1:]
    beams = steer_phase.shape[1]
    total = bins * lax.axis_size("range")
    slots = lax.axis_size("aperture")
    slot, column = lax.axis_index("aperture"), lax.axis_index("beam")
    axes = ("aperture", "beam")
    order = [z * 2 for z in range(slots)] + [z * 2 + 1 for z in reversed(range(slots))]
    ahead = [(order[i], order[(i + 1) % len(order)]) for i in range(len(order))]
    behind = [(b, a) for a, b in ahead]
    kind = jnp.where(column == 0, slot, slots - 1 - slot)
    half0, half1 = (bins + SPAN) // 2, bins // 2
    window = bins + 2 * SPAN

    core = lax.axis_index("range")

    def pairs(*pieces):
        rims = [jnp.where(core == 0, x[:, :, bins - LANES :], x[:, :, :LANES]) for x in pieces]
        rims = lax.ppermute(jnp.concatenate(rims, axis=0), "range", [(0, 1), (1, 0)])
        return [(x, rims[2 * i : 2 * i + 2]) for i, x in enumerate(pieces)]

    def choose(*options):
        picked = options[-1]
        for value, option in enumerate(options[:-1]):
            if option is not picked:
                picked = jnp.where(kind == value, option, picked)
        return picked

    vmem = pl.BlockSpec(memory_space=pltpu.VMEM)
    f32, bf16, i32 = jnp.float32, jnp.bfloat16, jnp.int32
    rows0 = NEAR + 2 * STEP + 2 * (half0 // STEP)
    rows1 = NEAR + 2 * STEP + 2 * (half1 // STEP)
    arguments = (chirp_taps, steer_phase, ang_table, range_table, interp_taps, phase_twist)
    tables = pl.pallas_call(
        functools.partial(table_kernel, total=total),
        out_shape=[
            jax.ShapeDtypeStruct((2 * LANES, 4 * LANES), bf16),
            jax.ShapeDtypeStruct((2 * SPAN, 2 * LANES), bf16),
            jax.ShapeDtypeStruct((4 * pulses, 2 * beams), bf16),
            jax.ShapeDtypeStruct((2, 2, 1, beams), i32),
            jax.ShapeDtypeStruct((2, 2, SUBS, LANES), i32),
            jax.ShapeDtypeStruct((2, rows0, SUBS, LANES), f32),
            jax.ShapeDtypeStruct((2, rows1, SUBS, LANES), f32),
        ],
        in_specs=[pl.BlockSpec(memory_space=pltpu.HBM)] * 6,
        out_specs=[vmem] * 7,
        scratch_shapes=[
            *(pltpu.VMEM(x.shape, x.dtype) for x in arguments),
            pltpu.VMEM((SUBS, 2 * LANES), f32),
            pltpu.SemaphoreType.DMA((len(arguments),)),
        ],
        compiler_params=pltpu.CompilerParams(vmem_limit_bytes=60 * 2**20),
        cost_estimate=pl.CostEstimate(flops=10**9, bytes_accessed=4 * 2**20, transcendentals=0),
        name="tables",
    )(*arguments)
    shared, table0, table1 = tables[:5], tables[5], tables[6]

    rows = (half0 + SPAN + 32) * SUBS
    squeezed = ((2, window, pulses), bf16)
    sums0, sums1 = ((half0 * SUBS, LANES), f32), ((half1 * SUBS, LANES), f32)
    image0, image1 = ((2, window, beams), bf16), ((2, window - SPAN, beams), bf16)
    rooms = [((rows, LANES), f32)] * 3

    def run(kernel, pieces, carried, out, scratch, place=vmem):
        given = [x for piece in pieces for x in piece] + [*shared, table0, *carried]
        return pl.pallas_call(
            functools.partial(kernel, total),
            out_shape=[jax.ShapeDtypeStruct(*x) for x in out],
            in_specs=[vmem] * len(given),
            out_specs=[place] * len(out),
            scratch_shapes=[pltpu.VMEM(*x) if isinstance(x, tuple) else x for x in scratch],
            compiler_params=pltpu.CompilerParams(vmem_limit_bytes=24 * 1024 * 1024),
            cost_estimate=pl.CostEstimate(
                flops=3 * 10**9, bytes_accessed=4 * 2**20, transcendentals=0
            ),
            name=kernel.__name__,
        )(*given)

    def after(value, result):
        return lax.optimization_barrier((value, result))[0]

    up1, down1 = lax.ppermute(echoes, axes, ahead), lax.ppermute(echoes, axes, behind)
    own = pairs(echoes)
    up1, down1 = after(up1, shared[0]), after(down1, shared[0])
    up2, down2 = lax.ppermute(up1, axes, ahead), lax.ppermute(down1, axes, behind)
    ready = pairs(choose(down1, up1, down1, up1), choose(up1, down1, up1, down1))
    up3, down3 = lax.ppermute(up2, axes, ahead), lax.ppermute(down2, axes, behind)
    fresh = pairs(choose(up2, up2, down2, down2), choose(down2, down2, up2, up2))
    part, c_own, c_next, c_early = run(
        first_stage,
        [ready[0], fresh[0], *own, fresh[1], ready[1]],
        [],
        [sums0, squeezed, squeezed, squeezed],
        [squeezed, squeezed, image0, *rooms],
    )
    up3, down3 = after(up3, part), after(down3, part)
    far_up, far_down = lax.ppermute(up3[:1], axes, ahead), lax.ppermute(down3[1:], axes, behind)
    near, c_b, c_late = run(
        second_stage,
        pairs(choose(down3, up3, down3, up3), choose(up3, down3, up3, down3)),
        [table1, part, c_own, c_early],
        [sums1, squeezed, squeezed],
        [image0, sums0, image1, *rooms],
    )
    far = pairs(jnp.concatenate([after(far_up, near), after(far_down, near)], axis=0))[0]
    other = run(third_stage, [], [c_next, c_b], [sums0], [image0, *rooms])[0]
    return run(
        last_stage,
        [(far[0], after(far[1], other))],
        [table1, near, other, c_early, c_late],
        [((1, 2, beams, bins), f32)],
        [
            squeezed,
            image0,
            sums0,
            image1,
            sums1,
            ((2, beams, bins), f32),
            pltpu.SemaphoreType.DMA((4,)),
            *rooms,
        ],
        pl.BlockSpec(memory_space=pl.ANY),
    )[0]


def solution(mesh):
    small = (mesh.shape["aperture"], mesh.shape["beam"], mesh.shape["range"]) == (4, 2, 2)
    return jax.shard_map(
        ring_of_chips if small else level_by_level,
        mesh=mesh,
        in_specs=(
            P(None, ("groups", "aperture", "beam"), "range"),
            P(),
            P(None, "beam"),
            P(None, None, None, "beam"),
            P(None, None, None, "beam"),
            P(None, None, None, None, None, "beam"),
            P(None, None, None, "beam"),
        ),
        out_specs=P(("groups", "aperture"), None, "beam", "range"),
        check_vma=False,
    )
```
